32 devices in a mesh: row: 4 (over y, core), col: 2 (over x), fib: 4 (over z).
Axes of the slice: x: 2, y: 2, z: 4, core: 2. Of those that a mesh axis runs over, the one named last changes fastest.
Arguments:
- values: bfloat16 [48, 12, 128, 128], P(('row', 'col'), 'fib'), may hold values from -3 to 3
- columns: int32 [48, 12], P(('row', 'col')), may hold values from 0 to 47, as said below
- counts: int32 [48], P(('row', 'col')), may hold values from 6 to 12, as said below
Outputs:
- square: bfloat16 [48, 12, 128, 128], P(('row', 'col'), 'fib')
- traces: float32 [2], replicated
The draws below stay inside these ranges and needn't reach their ends.
Inputs may be any that keep to these rules, and one draw needn't show every extreme that they name: Slot 0 of block row i holds i. Every slot s >= 1 of row i, used or not, holds (i + o) mod 48 with 1 <= |o| <= 6, and the columns of one row are distinct. Row i uses slots 0 to counts[i] - 1; later slots are ignored. Some row uses all 12 slots.
All inputs are finite; a program needn't handle non-finite values.
Results may differ from the reference program's by a relative error of at most 0.001.
Values may be sent and summed in bfloat16 or wider, within the bound.
No kernel may reach another device: no remote copies, remote signals or barrier semaphores. Data moves between devices by JAX's collectives and lax.ppermute only.
A program may use at most 128 MiB of HBM per device.

```python
import jax
import jax.numpy as jnp
from jax import lax

SLOTS = 12
BLOCK = 128
BAND = 6
NB = 48


def pattern_draw(key):
    base_key = jax.random.fold_in(key, 7)
    key_order, key_count, key_full, key_least = jax.random.split(base_key, 4)
    spread = 2 * BAND
    scores = jax.random.randint(key_order, (NB, spread), 0, 2 ** 20) * spread + jnp.arange(spread, dtype=jnp.int32)[None, :]
    ranked = jnp.argsort(scores, axis=1)[:, :SLOTS - 1].astype(jnp.int32)
    offsets = jnp.where(ranked < BAND, ranked - BAND, ranked - BAND + 1)
    row_ids = jnp.arange(NB, dtype=jnp.int32)[:, None]
    columns = jnp.concatenate([row_ids, (row_ids + offsets) % NB], axis=1).astype(jnp.int32)
    counts = jax.random.randint(key_count, (NB,), SLOTS // 2, SLOTS + 1).astype(jnp.int32)
    full_row = jax.random.randint(key_full, (), 0, NB)
    least_row = (full_row + 1 + jax.random.randint(key_least, (), 0, NB - 1)) % NB
    counts = counts.at[full_row].set(SLOTS).at[least_row].set(SLOTS // 2)
    return (columns, counts)


def draw_columns(key, part):
    return pattern_draw(key)[0]


def draw_counts(key, part):
    return pattern_draw(key)[1]


def draw_values(key, part):
    key_base = jax.random.fold_in(jax.random.fold_in(key, 3), 0)
    shape = (NB, SLOTS, BLOCK, BLOCK)
    entries = jax.random.normal(key_base, shape, jnp.float32) * 0.15
    rising = 0.5 + jnp.arange(NB, dtype=jnp.float32) / NB
    identity = jnp.eye(BLOCK, dtype=jnp.float32)
    entries = entries.at[:, 0].add(rising[:, None, None] * identity[None, :, :])
    return entries.astype(jnp.bfloat16)


def setup_inputs(seed: int = 0) -> dict:
    key_list = jax.random.split(jax.random.key(seed), 4)
    values = draw_values(jax.random.fold_in(key_list[3], 71), 0)
    columns = draw_columns(jax.random.fold_in(key_list[3], 71), 0)
    counts = draw_counts(jax.random.fold_in(key_list[3], 71), 0)
    return dict(values=values, columns=columns, counts=counts)


def reference(values, columns, counts):
    slot_count = columns.shape[1]
    slot_ids = jnp.arange(slot_count, dtype=jnp.int32)

    def one_row(row_id):
        row_cols = columns[row_id]
        keep_mask = slot_ids < counts[row_id]
        picked = values[row_cols].astype(jnp.float32)
        picked_cols = columns[row_cols]
        picked_live = slot_ids[None, :] < counts[row_cols][:, None]
        matches = (picked_cols[:, None, :] == row_cols[None, :, None]) & picked_live[:, None, :]
        matches = matches & keep_mask[:, None, None] & keep_mask[None, :, None]
        chosen = jnp.einsum("ajs,asxy->ajxy", matches.astype(jnp.float32), picked)
        left_tiles = values[row_id].astype(jnp.float32)
        product = jnp.einsum("axy,ajyz->jxz", left_tiles, chosen)
        trace_values = jnp.trace(left_tiles[0])
        trace_square = jnp.trace(product[0])
        return product.astype(jnp.bfloat16), trace_values, trace_square

    square, trace_values, trace_square = lax.map(one_row, jnp.arange(NB, dtype=jnp.int32))
    traces = jnp.stack([jnp.sum(trace_values), jnp.sum(trace_square)])
    return square, traces
```

```python
import functools

import jax
import jax.numpy as jnp
from jax import lax
from jax.experimental import pallas as pl
from jax.experimental.pallas import tpu as pltpu
from jax.sharding import PartitionSpec as P

BAND = 6
PLANE = ("row", "col")
ALL = ("row", "col", "fib")
NT = (((1,), (1,)), ((), ()))


def padded(array, sides, width):
    for axis, dim in sides:
        size, length = (lax.axis_size(axis), array.shape[dim])
        up = [(i, (i + 1) % size) for i in range(size)]
        down = [(j, i) for i, j in up]
        last = lax.slice_in_dim(array, length - width, length, axis=dim)
        initial = lax.slice_in_dim(array, 0, width, axis=dim)
        before = lax.ppermute(last, axis, up)
        after = lax.ppermute(initial, axis, down)
        array = jnp.concatenate([before, array, after], axis=dim)
    return array


def band_product(
    left_tiles, left_keep, fetch_index, target_cols, target_keep, window, window_cols, window_counts
):
    picked = jnp.take(window, fetch_index, axis=0)
    picked_cols = jnp.take(window_cols, fetch_index, axis=0)
    picked_counts = jnp.take(window_counts, fetch_index, axis=0)
    alive_slots = lax.broadcasted_iota(jnp.int32, picked_cols.shape, 1) < picked_counts[:, None]
    matches = (picked_cols[:, None, :] == target_cols[None, :, None]) & alive_slots[:, None, :]
    matches = matches & left_keep[:, None, None] & target_keep[None, :, None]
    chosen = jnp.einsum(
        "ajs,asxy->ajxy", matches.astype(jnp.bfloat16), picked, preferred_element_type=jnp.float32
    ).astype(jnp.bfloat16)
    return jnp.einsum("axy,ajyz->jxz", left_tiles, chosen, preferred_element_type=jnp.float32)


def general_body(values, columns, counts):
    rows_here = values.shape[0]
    share_count = values.shape[1]
    slot_count = columns.shape[1]
    block_total = rows_here * lax.axis_size(("row", "col"))
    fib_index = lax.axis_index("fib")
    full_rows = lax.all_gather(values, "fib", axis=1, tiled=True)
    window, window_cols, window_counts = (
        padded(full_rows, ((("row", "col"), 0),), BAND),
        padded(columns, ((("row", "col"), 0),), BAND),
        padded(counts, ((("row", "col"), 0),), BAND),
    )
    local_rows = jnp.arange(rows_here, dtype=jnp.int32)
    row_ids = lax.axis_index(("row", "col")) * rows_here + local_rows
    fetch_all = (columns - row_ids[:, None] + BAND) % block_total + local_rows[:, None]
    slot_ids = jnp.arange(slot_count, dtype=jnp.int32)
    keep_mask = slot_ids[None, :] < counts[:, None]
    first_slot = fib_index * share_count

    def one_row(operands):
        return band_product(*operands, window, window_cols, window_counts)

    own_rows = lax.dynamic_slice_in_dim(window, BAND, rows_here, 0)
    target_cols = lax.dynamic_slice_in_dim(columns, first_slot, share_count, 1)
    target_keep = lax.dynamic_slice_in_dim(keep_mask, first_slot, share_count, 1)
    product = lax.map(one_row, (own_rows, keep_mask, fetch_all, target_cols, target_keep))
    is_first = (fib_index == 0).astype(jnp.float32)
    trace_values = is_first * jnp.sum(
        jnp.diagonal(values[:, 0].astype(jnp.float32), axis1=1, axis2=2)
    )
    trace_square = is_first * jnp.sum(jnp.diagonal(product[:, 0], axis1=1, axis2=2))
    traces = lax.psum(jnp.stack([trace_values, trace_square]), ("row", "col", "fib"))
    return (product.astype(jnp.bfloat16), traces)


REACH = 64
NO_SLOT = 40
TAIL = 16


def vmem():
    return pl.BlockSpec(memory_space=pltpu.VMEM)


def smem():
    return pl.BlockSpec(memory_space=pltpu.SMEM)


def limit(mebibytes):
    return pltpu.CompilerParams(vmem_limit_bytes=mebibytes * 2**20)


def turn_kernel(half_ref, in_ref, out_ref):
    rows, share, block, _ = in_ref.shape
    width = block // 2
    z = lax.broadcasted_iota(jnp.int32, (width, block), 0) + half_ref[0] * width
    pick = (lax.broadcasted_iota(jnp.int32, (width, block), 1) == z).astype(jnp.bfloat16)
    for r in range(rows):
        for s in range(share):
            out_ref[r * share + s] = lax.dot_general(
                pick, in_ref[r, s], NT, preferred_element_type=jnp.float32
            ).astype(jnp.bfloat16)


def turned_half(half, slab):
    rows, share, block, _ = slab.shape
    return pl.pallas_call(
        turn_kernel,
        out_shape=jax.ShapeDtypeStruct((rows * share, block // 2, block), slab.dtype),
        in_specs=[smem(), vmem()],
        out_specs=vmem(),
        compiler_params=limit(6),
        name="turn",
    )(half, slab)


def product_kernel(rows, share, table_ref, place_ref, *refs):
    lefts, rights, outs = refs[:4], refs[4:16], refs[16:20]
    right, stacked = refs[20:]
    slots = 4 * share
    blocks = rows * share
    width, block = right.shape[1:]
    base_at = (3 * rows + 1) * REACH
    target_at = base_at + rows * slots
    for n in range(12):
        right[n * blocks : (n + 1) * blocks] = rights[n][...]
    right[12 * blocks] = jnp.zeros((width, block), right.dtype)

    half, is_low = place_ref[0], place_ref[1] == 1
    z = lax.broadcasted_iota(jnp.int32, (width, block), 0) + half * width
    on_diagonal = lax.broadcasted_iota(jnp.int32, (width, block), 1) == z
    start = pl.multiple_of(half * width, width)
    sum_values = jnp.zeros((width, block), jnp.float32)
    sum_square = jnp.zeros((width, block), jnp.float32)
    for r in range(rows):
        at = r % 2
        bases = [table_ref[base_at + r * slots + a] for a in range(slots)]
        targets = [table_ref[target_at + r * slots + j] for j in range(slots)]
        for j in range(slots):
            for a in range(slots):
                stacked[at, j * width : (j + 1) * width, a * block : (a + 1) * block] = right[
                    table_ref[bases[a] + targets[j]]
                ]
        left = jnp.concatenate([lefts[p][r, s] for p in range(4) for s in range(share)], axis=1)
        product = lax.dot_general(stacked[at], left, NT, preferred_element_type=jnp.float32)
        for p in range(4):
            for s in range(share):
                j = p * share + s
                outs[p][(r * share + s) * width : (r * share + s + 1) * width] = product[
                    j * width : (j + 1) * width
                ].astype(jnp.bfloat16)
        low, high = (product[j * width : (j + 1) * width] for j in (share, 3 * share))
        sum_square += jnp.where(is_low, low, high)
        low, high = (lefts[p][r, 0, pl.ds(start, width)].astype(jnp.float32) for p in (1, 3))
        sum_values += jnp.where(is_low, low, high)
    sums = [
        jnp.sum(jnp.where(on_diagonal, s, 0.0), axis=(0, 1), keepdims=True)
        for s in (sum_values, sum_square)
    ]
    lane = lax.broadcasted_iota(jnp.int32, (TAIL, block), 1)
    tail = jnp.zeros((TAIL, block), jnp.float32)
    for n, rest in enumerate(sums):
        for m in range(3):
            term = rest.astype(jnp.bfloat16).astype(jnp.float32)
            tail = jnp.where(lane == 2 * m + n, term, tail)
            rest = rest - term
    for out in outs:
        out[blocks * width :] = tail.astype(jnp.bfloat16)


def products(table, place, lefts, rights):
    rows, share, block, _ = lefts[0].shape
    width, slots = block // 2, 4 * share
    part = jax.ShapeDtypeStruct((rows * share * width + TAIL, block), jnp.bfloat16)
    flops = 2 * rows * slots * slots * width * block * block
    return pl.pallas_call(
        functools.partial(product_kernel, rows, share),
        out_shape=[part] * 4,
        in_specs=[smem(), smem()] + [vmem()] * 16,
        out_specs=[vmem()] * 4,
        scratch_shapes=[
            pltpu.VMEM((12 * rows * share + 1, width, block), jnp.bfloat16),
            pltpu.VMEM((2, slots * width, slots * block), jnp.bfloat16),
        ],
        compiler_params=limit(32),
        cost_estimate=pl.CostEstimate(flops=flops, bytes_accessed=8 * 2**20, transcendentals=0),
        name="products",
    )(table, place, *lefts, *rights)


PLANE_PARTS = ((1, 3), (0, 2), (2, 0), (3, 1))


def add_kernel(fib_ref, own_ref, near_ref, mid_ref, far_ref, out_ref):
    parts = (own_ref, near_ref, mid_ref, far_ref)

    def write(*pair):
        first, second = (p[p.shape[0] - TAIL :].astype(jnp.float32) for p in pair)
        lane = lax.broadcasted_iota(jnp.int32, first.shape, 1)
        totals = []
        for n in range(2):
            terms = [
                [
                    jnp.sum(jnp.where(lane == 2 * m + n, p, 0.0), axis=1, keepdims=True)
                    for m in range(3)
                ]
                for p in (first, second)
            ]
            a, b = (t[0] + (t[1] + t[2]) for t in terms)
            totals.append(a + b)
        total = jnp.where(lane == 0, totals[0], jnp.where(lane == 1, totals[1], 0.0))
        out_ref[...] = total[:8]

    for plane, pair in enumerate(PLANE_PARTS):
        pl.when(fib_ref[0] == plane)(functools.partial(write, *(parts[n] for n in pair)))


def added(fib, parts):
    return pl.pallas_call(
        add_kernel,
        out_shape=jax.ShapeDtypeStruct((8, 128), jnp.float32),
        in_specs=[smem()] + [vmem()] * 4,
        out_specs=vmem(),
        compiler_params=limit(6),
        name="add",
    )(fib, *parts)


def join_kernel(fib_ref, own_ref, near_ref, mid_ref, far_ref, out_ref):
    rows, share, block, _ = out_ref.shape
    width = block // 2
    parts = (own_ref, near_ref, mid_ref, far_ref)

    def write(*pair):
        for r in range(rows):
            for s in range(share):
                n = r * share + s
                halves = [p[n * width : (n + 1) * width] for p in pair]
                out_ref[r, s] = jnp.concatenate(halves, axis=0).T

    for plane, pair in enumerate(PLANE_PARTS):
        pl.when(fib_ref[0] == plane)(functools.partial(write, *(parts[n] for n in pair)))


def joined(fib, parts, rows, share):
    block = parts[0].shape[1]
    return pl.pallas_call(
        join_kernel,
        out_shape=jax.ShapeDtypeStruct((rows, share, block, block), parts[0].dtype),
        in_specs=[smem()] + [vmem()] * 4,
        out_specs=vmem(),
        compiler_params=limit(8),
        name="join",
    )(fib, *parts)


def middle_body(groups, values, columns, counts):
    rows, share, block, _ = values.shape
    slots = columns.shape[1]
    fib = lax.axis_index("fib")
    group = lax.axis_index(PLANE)
    high = fib >= 2

    low_order, high_order = (1, 0, 2, 3), (2, 3, 1, 0)
    inward = [[(0, 1), (3, 2)], [(1, 2), (2, 1)], [(0, 2), (3, 1)]]
    outward = [[(j, i) for i, j in pairs] for pairs in inward]

    def middle(pairs):
        return [(i * 4 + f, j * 4 + f) for i, j in pairs for f in (1, 2)]

    swap = [(i, i ^ 1) for i in range(groups)]
    skip = [((i + 2) % groups if i % 2 else (i - 2) % groups, i) for i in range(groups)]

    def from_both(array):
        first = lax.ppermute(array, PLANE, swap)
        return first, lax.ppermute(first, PLANE, skip)

    def from_both_middle(array):
        first = lax.ppermute(array, ALL, middle(swap))
        return first, lax.ppermute(first, ALL, middle(skip))

    near, mid, far = (lax.ppermute(values, "fib", pairs) for pairs in inward)

    half = jnp.where(high, 1, 0).astype(jnp.int32).reshape(1)
    own_half = (1 - fib % 2).astype(jnp.int32).reshape(1)
    own_turned = turned_half(own_half, values)
    own_around = from_both(own_turned)
    far_around = tuple(lax.ppermute(a, "fib", inward[2]) for a in own_around)
    near_turned, mid_turned, far_turned = (turned_half(half, slab) for slab in (near, mid, far))
    near_around = from_both_middle(near_turned)
    mid_around = from_both_middle(mid_turned)
    rights = [own_turned, near_turned, mid_turned, far_turned]
    for n in range(2):
        rights += [own_around[n], near_around[n], mid_around[n], far_around[n]]

    def in_order(array):
        cut = [array[:, p * share : (p + 1) * share] for p in range(4)]
        low, up = (jnp.concatenate([cut[p] for p in o], axis=1) for o in (low_order, high_order))
        return jnp.where(high, up, low)

    row_ids = jnp.arange(rows, dtype=jnp.int32)[:, None]
    slot_ids = jnp.arange(slots, dtype=jnp.int32)[None, :]
    total = groups * rows
    mine = in_order(columns)
    used = in_order((slot_ids < counts[:, None]).astype(jnp.int32)) > 0
    distance = (mine - (group * rows + row_ids) + BAND + total) % total - BAND
    block_index = (slot_ids // share * rows + row_ids) * share + slot_ids % share
    reach = jnp.arange(REACH, dtype=jnp.int32)[None, None, :]
    hit = used[:, :, None] & (distance[:, :, None] + 2 * BAND == reach)
    found = jnp.sum(jnp.where(hit, block_index[:, :, None] + 1, 0), axis=1) - 1
    found_around = from_both(found)
    nothing = 12 * rows * share
    lists = [
        jnp.where(f < 0, nothing, f + n * 4 * rows * share)
        for n, f in enumerate((found, *found_around))
    ]
    lists.append(jnp.full((1, REACH), nothing, jnp.int32))
    owner = mine // rows
    which = jnp.where(owner == group, 0, jnp.where(owner == (group ^ 1), 1, 2))
    base = (which * rows + mine % rows) * REACH - distance + 2 * BAND
    base = jnp.where(used, base, 3 * rows * REACH + 2 * BAND)
    target = jnp.where(used, distance, NO_SLOT)
    table = jnp.concatenate(
        [x.reshape(-1).astype(jnp.int32) for x in (*lists, base, target)], axis=0
    )

    place = jnp.stack([jnp.where(high, 1, 0), jnp.where(high, 0, 1)]).astype(jnp.int32)
    parts = products(table, place, [values, near, mid, far], rights)
    parts = [parts[0]] + [
        lax.ppermute(o, "fib", pairs) for o, pairs in zip(parts[1:], outward)
    ]
    fib_ref = fib.reshape(1).astype(jnp.int32)
    sums = added(fib_ref, parts)
    square = joined(fib_ref, parts, rows, share)

    def moved(array, bits):
        return lax.ppermute(array, PLANE, [(i, i ^ bits) for i in range(groups)])

    bits = [1 << n for n in range(groups.bit_length() - 1)]
    if len(bits) % 2:
        alone = bits.pop(len(bits) // 2)
        sums = sums + moved(sums, alone)
    while bits:
        one, two = bits.pop(0), bits.pop()
        a, b, c = moved(sums, one), moved(sums, two), moved(sums, one | two)
        sums = (sums + a) + (b + c)
    return square, sums[0, :2]


def solution(mesh):
    in_specs = (P(("row", "col"), "fib", None, None), P(("row", "col"), None), P(("row", "col")))
    out_specs = (P(("row", "col"), "fib", None, None), P())
    groups = mesh.shape["row"] * mesh.shape["col"]

    def body(values, columns, counts):
        fits = groups >= 4 and groups & (groups - 1) == 0 and mesh.shape["fib"] == 4
        if fits and values.shape[0] >= BAND:
            return middle_body(groups, values, columns, counts)
        return general_body(values, columns, counts)

    return jax.shard_map(body, mesh=mesh, in_specs=in_specs, out_specs=out_specs, check_vma=False)
```

```python
import functools

import jax
import jax.numpy as jnp
from jax import lax
from jax.experimental import pallas as pl
from jax.experimental.pallas import tpu as pltpu
from jax.sharding import PartitionSpec as P

BAND = 6
PLANE = ("row", "col")
ALL = ("row", "col", "fib")
NT = (((1,), (1,)), ((), ()))


def padded(array, sides, width):
    for axis, dim in sides:
        size, length = (lax.axis_size(axis), array.shape[dim])
        up = [(i, (i + 1) % size) for i in range(size)]
        down = [(j, i) for i, j in up]
        last = lax.slice_in_dim(array, length - width, length, axis=dim)
        initial = lax.slice_in_dim(array, 0, width, axis=dim)
        before = lax.ppermute(last, axis, up)
        after = lax.ppermute(initial, axis, down)
        array = jnp.concatenate([before, array, after], axis=dim)
    return array


def band_product(
    left_tiles, left_keep, fetch_index, target_cols, target_keep, window, window_cols, window_counts
):
    picked = jnp.take(window, fetch_index, axis=0)
    picked_cols = jnp.take(window_cols, fetch_index, axis=0)
    picked_counts = jnp.take(window_counts, fetch_index, axis=0)
    alive_slots = lax.broadcasted_iota(jnp.int32, picked_cols.shape, 1) < picked_counts[:, None]
    matches = (picked_cols[:, None, :] == target_cols[None, :, None]) & alive_slots[:, None, :]
    matches = matches & left_keep[:, None, None] & target_keep[None, :, None]
    chosen = jnp.einsum(
        "ajs,asxy->ajxy", matches.astype(jnp.bfloat16), picked, preferred_element_type=jnp.float32
    ).astype(jnp.bfloat16)
    return jnp.einsum("axy,ajyz->jxz", left_tiles, chosen, preferred_element_type=jnp.float32)


def general_body(values, columns, counts):
    rows_here = values.shape[0]
    share_count = values.shape[1]
    slot_count = columns.shape[1]
    block_total = rows_here * lax.axis_size(("row", "col"))
    fib_index = lax.axis_index("fib")
    full_rows = lax.all_gather(values, "fib", axis=1, tiled=True)
    window, window_cols, window_counts = (
        padded(full_rows, ((("row", "col"), 0),), BAND),
        padded(columns, ((("row", "col"), 0),), BAND),
        padded(counts, ((("row", "col"), 0),), BAND),
    )
    local_rows = jnp.arange(rows_here, dtype=jnp.int32)
    row_ids = lax.axis_index(("row", "col")) * rows_here + local_rows
    fetch_all = (columns - row_ids[:, None] + BAND) % block_total + local_rows[:, None]
    slot_ids = jnp.arange(slot_count, dtype=jnp.int32)
    keep_mask = slot_ids[None, :] < counts[:, None]
    first_slot = fib_index * share_count

    def one_row(operands):
        return band_product(*operands, window, window_cols, window_counts)

    own_rows = lax.dynamic_slice_in_dim(window, BAND, rows_here, 0)
    target_cols = lax.dynamic_slice_in_dim(columns, first_slot, share_count, 1)
    target_keep = lax.dynamic_slice_in_dim(keep_mask, first_slot, share_count, 1)
    product = lax.map(one_row, (own_rows, keep_mask, fetch_all, target_cols, target_keep))
    is_first = (fib_index == 0).astype(jnp.float32)
    trace_values = is_first * jnp.sum(
        jnp.diagonal(values[:, 0].astype(jnp.float32), axis1=1, axis2=2)
    )
    trace_square = is_first * jnp.sum(jnp.diagonal(product[:, 0], axis1=1, axis2=2))
    traces = lax.psum(jnp.stack([trace_values, trace_square]), ("row", "col", "fib"))
    return (product.astype(jnp.bfloat16), traces)


REACH = 64
NO_SLOT = 40
TAIL = 16


def vmem():
    return pl.BlockSpec(memory_space=pltpu.VMEM)


def smem():
    return pl.BlockSpec(memory_space=pltpu.SMEM)


def limit(mebibytes):
    return pltpu.CompilerParams(vmem_limit_bytes=mebibytes * 2**20)


def turn_kernel(half_ref, in_ref, out_ref):
    blocks, width, block = out_ref.shape
    z = lax.broadcasted_iota(jnp.int32, (width, block), 0) + half_ref[0] * width
    pick = (lax.broadcasted_iota(jnp.int32, (width, block), 1) == z).astype(jnp.bfloat16)
    for n in range(blocks):
        out_ref[n] = lax.dot_general(
            pick, in_ref[n * block : (n + 1) * block], NT, preferred_element_type=jnp.float32
        ).astype(jnp.bfloat16)


def turned_half(half, slab, blocks):
    block = slab.shape[1]
    return pl.pallas_call(
        turn_kernel,
        out_shape=jax.ShapeDtypeStruct((blocks, block // 2, block), slab.dtype),
        in_specs=[smem(), vmem()],
        out_specs=vmem(),
        compiler_params=limit(8),
        name="turn",
    )(half, slab)


def pack_kernel(slab_ref, first_ref, second_ref, out_ref):
    blocks, width, _ = first_ref.shape
    at = slab_ref.shape[0]
    out_ref[:at] = slab_ref[...]
    for halves in (first_ref, second_ref):
        for n in range(blocks):
            out_ref[at : at + width] = halves[n]
            at += width


def packed(slab, first, second):
    return pl.pallas_call(
        pack_kernel,
        out_shape=jax.ShapeDtypeStruct((2 * slab.shape[0], slab.shape[1]), slab.dtype),
        in_specs=[vmem()] * 3,
        out_specs=vmem(),
        compiler_params=limit(8),
        name="pack",
    )(slab, first, second)


def product_kernel(sizes, chunk, with_tail, table_ref, place_ref, *refs):
    rows, share = sizes
    lefts, rights, outs = refs[:4], refs[4:14], refs[14:18]
    right, stacked = refs[18:]
    slots = 4 * share
    blocks = rows * share
    width, block = right.shape[1:]
    base_at = (3 * rows + 1) * REACH
    target_at = base_at + rows * slots
    for n in range(10):
        right[n * blocks : (n + 1) * blocks] = rights[n][...]
    for n in range(2 * blocks):
        at = blocks * block + n * width
        right[10 * blocks + n] = lefts[3][at : at + width]
    right[12 * blocks] = jnp.zeros((width, block), right.dtype)

    half, is_low = place_ref[0], place_ref[1] == 1
    start = pl.multiple_of(half * width, width)

    def bases_of(r):
        return [table_ref[base_at + r * slots + a] for a in range(slots)]

    def left_at(a, r, offset, size):
        at = (r * share + a % share) * block
        return lefts[a // share][pl.ds(at + offset, size)]

    for n, r in enumerate(chunk):
        at = n % 2
        bases = bases_of(r)
        targets = [table_ref[target_at + r * slots + j] for j in range(slots)]
        for j in range(slots):
            for a in range(slots):
                stacked[at, j * width : (j + 1) * width, a * block : (a + 1) * block] = right[
                    table_ref[bases[a] + targets[j]]
                ]
        left = jnp.concatenate([left_at(a, r, 0, block) for a in range(slots)], axis=1)
        product = lax.dot_general(stacked[at], left, NT, preferred_element_type=jnp.float32)
        for p in range(4):
            for s in range(share):
                j = p * share + s
                outs[p][(n * share + s) * width : (n * share + s + 1) * width] = product[
                    j * width : (j + 1) * width
                ].astype(jnp.bfloat16)
    if not with_tail:
        return

    z = lax.broadcasted_iota(jnp.int32, (width, block), 0) + half * width
    on_diagonal = lax.broadcasted_iota(jnp.int32, (width, block), 1) == z
    sum_values = jnp.zeros((width, block), jnp.float32)
    sum_square = jnp.zeros((width, block), jnp.float32)
    for r in range(rows):
        bases = bases_of(r)
        for a in range(slots):
            other = right[table_ref[bases[a]]]
            mine = left_at(a, r, start, width)
            sum_square += mine.astype(jnp.float32) * other.astype(jnp.float32)
        low, high = (left_at(a, r, start, width).astype(jnp.float32) for a in (share, 3 * share))
        sum_values += jnp.where(on_diagonal, jnp.where(is_low, low, high), 0.0)
    sums = [jnp.sum(s, axis=(0, 1), keepdims=True) for s in (sum_values, sum_square)]
    lane = lax.broadcasted_iota(jnp.int32, (TAIL, block), 1)
    tail = jnp.zeros((TAIL, block), jnp.float32)
    for n, rest in enumerate(sums):
        for m in range(3):
            term = rest.astype(jnp.bfloat16).astype(jnp.float32)
            tail = jnp.where(lane == 2 * m + n, term, tail)
            rest = rest - term
    for out in outs:
        out[len(chunk) * share * width :] = tail.astype(jnp.bfloat16)


def products(sizes, chunk, with_tail, table, place, lefts, rights):
    rows, share = sizes
    block = lefts[0].shape[1]
    width, slots = block // 2, 4 * share
    length = len(chunk) * share * width + (TAIL if with_tail else 0)
    part = jax.ShapeDtypeStruct((length, block), jnp.bfloat16)
    flops = 2 * len(chunk) * slots * slots * width * block * block
    return pl.pallas_call(
        functools.partial(product_kernel, sizes, chunk, with_tail),
        out_shape=[part] * 4,
        in_specs=[smem(), smem()] + [vmem()] * 14,
        out_specs=[vmem()] * 4,
        scratch_shapes=[
            pltpu.VMEM((12 * rows * share + 1, width, block), jnp.bfloat16),
            pltpu.VMEM((2, slots * width, slots * block), jnp.bfloat16),
        ],
        compiler_params=limit(32),
        cost_estimate=pl.CostEstimate(flops=flops, bytes_accessed=4 * 2**20, transcendentals=0),
        name="products",
    )(table, place, *lefts, *rights)


PLANE_PARTS = ((1, 3), (0, 2), (2, 0), (3, 1))


def add_kernel(fib_ref, own_ref, near_ref, mid_ref, far_ref, out_ref):
    parts = (own_ref, near_ref, mid_ref, far_ref)

    def write(*pair):
        first, second = (p[p.shape[0] - TAIL :].astype(jnp.float32) for p in pair)
        lane = lax.broadcasted_iota(jnp.int32, first.shape, 1)
        totals = []
        for n in range(2):
            terms = [
                [
                    jnp.sum(jnp.where(lane == 2 * m + n, p, 0.0), axis=1, keepdims=True)
                    for m in range(3)
                ]
                for p in (first, second)
            ]
            a, b = (t[0] + (t[1] + t[2]) for t in terms)
            totals.append(a + b)
        total = jnp.where(lane == 0, totals[0], jnp.where(lane == 1, totals[1], 0.0))
        out_ref[...] = total[:8]

    for plane, pair in enumerate(PLANE_PARTS):
        pl.when(fib_ref[0] == plane)(functools.partial(write, *(parts[n] for n in pair)))


def added(fib, parts):
    return pl.pallas_call(
        add_kernel,
        out_shape=jax.ShapeDtypeStruct((8, 128), jnp.float32),
        in_specs=[smem()] + [vmem()] * 4,
        out_specs=vmem(),
        compiler_params=limit(6),
        name="add",
    )(fib, *parts)


def join_kernel(chunks, fib_ref, *refs):
    out_ref = refs[-1]
    share, block = out_ref.shape[1:3]
    width = block // 2

    def write(*pair):
        for c, chunk in enumerate(chunks):
            for n, r in enumerate(chunk):
                for s in range(share):
                    at = (n * share + s) * width
                    halves = [refs[4 * c + p][at : at + width] for p in pair]
                    out_ref[r, s] = jnp.concatenate(halves, axis=0).T

    for plane, pair in enumerate(PLANE_PARTS):
        pl.when(fib_ref[0] == plane)(functools.partial(write, *pair))


def joined(sizes, chunks, fib, parts):
    block = parts[0].shape[1]
    return pl.pallas_call(
        functools.partial(join_kernel, chunks),
        out_shape=jax.ShapeDtypeStruct((*sizes, block, block), parts[0].dtype),
        in_specs=[smem()] + [vmem()] * len(parts),
        out_specs=vmem(),
        compiler_params=limit(8),
        name="join",
    )(fib, *parts)


def middle_body(groups, values, columns, counts):
    rows, share, block, _ = values.shape
    slots = columns.shape[1]
    fib = lax.axis_index("fib")
    group = lax.axis_index(PLANE)
    high = fib >= 2

    low_order, high_order = (1, 0, 2, 3), (2, 3, 1, 0)
    inward = [[(0, 1), (3, 2)], [(1, 2), (2, 1)], [(0, 2), (3, 1)]]
    outward = [[(j, i) for i, j in pairs] for pairs in inward]

    def middle(pairs):
        return [(i * 4 + f, j * 4 + f) for i, j in pairs for f in (1, 2)]

    swap = [(i, i ^ 1) for i in range(groups)]
    skip = [((i + 2) % groups if i % 2 else (i - 2) % groups, i) for i in range(groups)]

    def from_both(array):
        first = lax.ppermute(array, PLANE, swap)
        return first, lax.ppermute(first, PLANE, skip)

    def from_both_middle(array):
        first = lax.ppermute(array, ALL, middle(swap))
        return first, lax.ppermute(first, ALL, middle(skip))

    flat = values.reshape(rows * share * block, block)
    near, mid = (lax.ppermute(flat, "fib", pairs) for pairs in inward[:2])

    half = jnp.where(high, 1, 0).astype(jnp.int32).reshape(1)
    own_half = (1 - fib % 2).astype(jnp.int32).reshape(1)
    own_turned = turned_half(own_half, flat, rows * share)
    own_around = from_both(own_turned)
    far = lax.ppermute(packed(flat, *own_around), "fib", inward[2])
    near_turned, mid_turned, far_turned = (
        turned_half(half, slab, rows * share) for slab in (near, mid, far)
    )
    near_around = from_both_middle(near_turned)
    mid_around = from_both_middle(mid_turned)
    rights = [own_turned, near_turned, mid_turned, far_turned]
    for n in range(2):
        rights += [own_around[n], near_around[n], mid_around[n]]

    def in_order(array):
        cut = [array[:, p * share : (p + 1) * share] for p in range(4)]
        low, up = (jnp.concatenate([cut[p] for p in o], axis=1) for o in (low_order, high_order))
        return jnp.where(high, up, low)

    row_ids = jnp.arange(rows, dtype=jnp.int32)[:, None]
    slot_ids = jnp.arange(slots, dtype=jnp.int32)[None, :]
    total = groups * rows
    mine = in_order(columns)
    used = in_order((slot_ids < counts[:, None]).astype(jnp.int32)) > 0
    distance = (mine - (group * rows + row_ids) + BAND + total) % total - BAND
    block_index = (slot_ids // share * rows + row_ids) * share + slot_ids % share
    reach = jnp.arange(REACH, dtype=jnp.int32)[None, None, :]
    hit = used[:, :, None] & (distance[:, :, None] + 2 * BAND == reach)
    found = jnp.sum(jnp.where(hit, block_index[:, :, None] + 1, 0), axis=1) - 1
    found_around = from_both(found)
    blocks = rows * share
    nothing = 12 * blocks
    lists = [jnp.where(found < 0, nothing, found)]
    for n, f in enumerate(found_around):
        at = jnp.where(f < 3 * blocks, (4 + 3 * n) * blocks, (7 + n) * blocks)
        lists.append(jnp.where(f < 0, nothing, f + at))
    lists.append(jnp.full((1, REACH), nothing, jnp.int32))
    owner = mine // rows
    which = jnp.where(owner == group, 0, jnp.where(owner == (group ^ 1), 1, 2))
    base = (which * rows + mine % rows) * REACH - distance + 2 * BAND
    base = jnp.where(used, base, 3 * rows * REACH + 2 * BAND)
    target = jnp.where(used, distance, NO_SLOT)
    table = jnp.concatenate(
        [x.reshape(-1).astype(jnp.int32) for x in (*lists, base, target)], axis=0
    )

    place = jnp.stack([jnp.where(high, 1, 0), jnp.where(high, 0, 1)]).astype(jnp.int32)
    sizes = (rows, share)
    chunks = (range(rows // 2), range(rows // 2, rows))
    gathered = []
    for n, chunk in enumerate(chunks):
        parts = products(sizes, chunk, n == 0, table, place, [flat, near, mid, far], rights)
        gathered += [parts[0]] + [
            lax.ppermute(o, "fib", pairs) for o, pairs in zip(parts[1:], outward)
        ]
    fib_ref = fib.reshape(1).astype(jnp.int32)
    sums = added(fib_ref, gathered[:4])
    square = joined(sizes, chunks, fib_ref, gathered)

    def moved(array, bits):
        return lax.ppermute(array, PLANE, [(i, i ^ bits) for i in range(groups)])

    bits = [1 << n for n in range(groups.bit_length() - 1)]
    if len(bits) % 2:
        alone = bits.pop(len(bits) // 2)
        sums = sums + moved(sums, alone)
    while bits:
        one, two = bits.pop(0), bits.pop()
        a, b, c = moved(sums, one), moved(sums, two), moved(sums, one | two)
        sums = (sums + a) + (b + c)
    return square, sums[0, :2]


def solution(mesh):
    in_specs = (P(("row", "col"), "fib", None, None), P(("row", "col"), None), P(("row", "col")))
    out_specs = (P(("row", "col"), "fib", None, None), P())
    groups = mesh.shape["row"] * mesh.shape["col"]

    def body(values, columns, counts):
        fits = groups >= 4 and groups & (groups - 1) == 0 and mesh.shape["fib"] == 4
        if fits and values.shape[0] >= BAND:
            return middle_body(groups, values, columns, counts)
        return general_body(values, columns, counts)

    return jax.shard_map(body, mesh=mesh, in_specs=in_specs, out_specs=out_specs, check_vma=False)
```

```python
import functools

import jax
import jax.numpy as jnp
from jax import lax
from jax.experimental import pallas as pl
from jax.experimental.pallas import tpu as pltpu
from jax.sharding import PartitionSpec as P

BAND = 6
PLANE = ("row", "col")
ALL = ("row", "col", "fib")
NT = (((1,), (1,)), ((), ()))


def padded(array, sides, width):
    for axis, dim in sides:
        size, length = (lax.axis_size(axis), array.shape[dim])
        up = [(i, (i + 1) % size) for i in range(size)]
        down = [(j, i) for i, j in up]
        last = lax.slice_in_dim(array, length - width, length, axis=dim)
        initial = lax.slice_in_dim(array, 0, width, axis=dim)
        before = lax.ppermute(last, axis, up)
        after = lax.ppermute(initial, axis, down)
        array = jnp.concatenate([before, array, after], axis=dim)
    return array


def band_product(
    left_tiles, left_keep, fetch_index, target_cols, target_keep, window, window_cols, window_counts
):
    picked = jnp.take(window, fetch_index, axis=0)
    picked_cols = jnp.take(window_cols, fetch_index, axis=0)
    picked_counts = jnp.take(window_counts, fetch_index, axis=0)
    alive_slots = lax.broadcasted_iota(jnp.int32, picked_cols.shape, 1) < picked_counts[:, None]
    matches = (picked_cols[:, None, :] == target_cols[None, :, None]) & alive_slots[:, None, :]
    matches = matches & left_keep[:, None, None] & target_keep[None, :, None]
    chosen = jnp.einsum(
        "ajs,asxy->ajxy", matches.astype(jnp.bfloat16), picked, preferred_element_type=jnp.float32
    ).astype(jnp.bfloat16)
    return jnp.einsum("axy,ajyz->jxz", left_tiles, chosen, preferred_element_type=jnp.float32)


def general_body(values, columns, counts):
    rows_here = values.shape[0]
    share_count = values.shape[1]
    slot_count = columns.shape[1]
    block_total = rows_here * lax.axis_size(("row", "col"))
    fib_index = lax.axis_index("fib")
    full_rows = lax.all_gather(values, "fib", axis=1, tiled=True)
    window, window_cols, window_counts = (
        padded(full_rows, ((("row", "col"), 0),), BAND),
        padded(columns, ((("row", "col"), 0),), BAND),
        padded(counts, ((("row", "col"), 0),), BAND),
    )
    local_rows = jnp.arange(rows_here, dtype=jnp.int32)
    row_ids = lax.axis_index(("row", "col")) * rows_here + local_rows
    fetch_all = (columns - row_ids[:, None] + BAND) % block_total + local_rows[:, None]
    slot_ids = jnp.arange(slot_count, dtype=jnp.int32)
    keep_mask = slot_ids[None, :] < counts[:, None]
    first_slot = fib_index * share_count

    def one_row(operands):
        return band_product(*operands, window, window_cols, window_counts)

    own_rows = lax.dynamic_slice_in_dim(window, BAND, rows_here, 0)
    target_cols = lax.dynamic_slice_in_dim(columns, first_slot, share_count, 1)
    target_keep = lax.dynamic_slice_in_dim(keep_mask, first_slot, share_count, 1)
    product = lax.map(one_row, (own_rows, keep_mask, fetch_all, target_cols, target_keep))
    is_first = (fib_index == 0).astype(jnp.float32)
    trace_values = is_first * jnp.sum(
        jnp.diagonal(values[:, 0].astype(jnp.float32), axis1=1, axis2=2)
    )
    trace_square = is_first * jnp.sum(jnp.diagonal(product[:, 0], axis1=1, axis2=2))
    traces = lax.psum(jnp.stack([trace_values, trace_square]), ("row", "col", "fib"))
    return (product.astype(jnp.bfloat16), traces)


LANES = 128
NO_SLOT = 40
TAIL = 16


def vmem():
    return pl.BlockSpec(memory_space=pltpu.VMEM)


def smem():
    return pl.BlockSpec(memory_space=pltpu.SMEM)


def limit(mebibytes):
    return pltpu.CompilerParams(vmem_limit_bytes=mebibytes * 2**20)


LOW_PLACE, HIGH_PLACE = (1, 0, 2, 3), (3, 2, 0, 1)


def turn_kernel(half_ref, in_ref, out_ref):
    blocks, width, block = out_ref.shape
    z = lax.broadcasted_iota(jnp.int32, (width, block), 0) + half_ref[0] * width
    pick = (lax.broadcasted_iota(jnp.int32, (width, block), 1) == z).astype(jnp.bfloat16)
    for n in range(blocks):
        out_ref[n] = lax.dot_general(
            pick, in_ref[n * block : (n + 1) * block], NT, preferred_element_type=jnp.float32
        ).astype(jnp.bfloat16)


def turned_half(half, slab, blocks):
    block = slab.shape[1]
    return pl.pallas_call(
        turn_kernel,
        out_shape=jax.ShapeDtypeStruct((blocks, block // 2, block), slab.dtype),
        in_specs=[smem(), vmem()],
        out_specs=vmem(),
        compiler_params=limit(8),
        name="turn",
    )(half, slab)


def pack_kernel(first_ref, second_ref, out_ref):
    out_ref[0] = first_ref[...]
    out_ref[1] = second_ref[...]


def packed(first, second):
    return pl.pallas_call(
        pack_kernel,
        out_shape=jax.ShapeDtypeStruct((2, *first.shape), first.dtype),
        in_specs=[vmem()] * 2,
        out_specs=vmem(),
        compiler_params=limit(8),
        name="pack",
    )(first, second)


def slots_of(group_ref, counts_ref, columns_ref, groups):
    rows, slots = columns_ref.shape
    row = lax.broadcasted_iota(jnp.int32, (rows, slots), 0)
    count = jnp.zeros((rows, slots), jnp.int32)
    for r in range(rows):
        count = jnp.where(row == r, counts_ref[r], count)
    used = lax.broadcasted_iota(jnp.int32, (rows, slots), 1) < count
    total = groups * rows
    distance = columns_ref[...] - (group_ref[0] * rows + row)
    distance = jnp.where(distance > BAND, distance - total, distance)
    distance = jnp.where(distance < -BAND, distance + total, distance)
    return row, used, distance


def find_kernel(groups, group_ref, counts_ref, columns_ref, out_ref):
    rows, slots = columns_ref.shape
    share = slots // 4
    _, used, distance = slots_of(group_ref, counts_ref, columns_ref, groups)
    at = jnp.where(used, distance + 2 * BAND, LANES)
    lane = lax.broadcasted_iota(jnp.int32, (rows, LANES), 1)
    row = lax.broadcasted_iota(jnp.int32, (rows, LANES), 0)
    found = jnp.full((rows, LANES), -1, jnp.int32)
    for s in range(slots):
        p = jnp.where(group_ref[1] == 1, HIGH_PLACE[s // share], LOW_PLACE[s // share])
        found = jnp.where(at[:, s : s + 1] == lane, (p * rows + row) * share + s % share, found)
    out_ref[...] = found


def table_kernel(groups, group_ref, counts_ref, columns_ref, own_ref, first_ref, second_ref, out_ref):
    rows, slots = columns_ref.shape
    count = slots // 4 * rows
    nothing = 12 * count
    row, used, distance = slots_of(group_ref, counts_ref, columns_ref, groups)
    out_ref[...] = jnp.full(out_ref.shape, nothing, jnp.int32)
    for n, ref in enumerate((own_ref, first_ref, second_ref)):
        found = ref[...]
        out_ref[n * rows : (n + 1) * rows] = jnp.where(
            found < 0, nothing, found + n * 4 * count
        )
    to = row + distance
    even = group_ref[0] % 2 == 0
    after = jnp.where(even, rows, 2 * rows) - rows
    before = jnp.where(even, 2 * rows, rows) + rows
    to = jnp.where(to >= rows, to + after, jnp.where(to < 0, to + before, to))
    base = to * LANES - distance + 2 * BAND
    base = jnp.where(used, base, 3 * rows * LANES + 2 * BAND)
    out_ref[3 * rows + 1 : 4 * rows + 1, :slots] = base
    out_ref[4 * rows + 1 : 5 * rows + 1, :slots] = jnp.where(used, distance, NO_SLOT)


def slot_table(groups, group, columns, counts, exchange):
    rows = columns.shape[0]
    params = dict(out_specs=vmem(), compiler_params=limit(2))
    found = pl.pallas_call(
        functools.partial(find_kernel, groups),
        out_shape=jax.ShapeDtypeStruct((rows, LANES), jnp.int32),
        in_specs=[smem(), smem(), vmem()],
        name="find",
        **params,
    )(group, counts, columns)
    first, second = exchange(found)
    height = -(-(5 * rows + 1) // 8) * 8
    table = pl.pallas_call(
        functools.partial(table_kernel, groups),
        out_shape=jax.ShapeDtypeStruct((height, LANES), jnp.int32),
        in_specs=[smem(), smem()] + [vmem()] * 4,
        name="table",
        **params,
    )(group, counts, columns, found, first, second)
    return table.reshape(-1)


def product_kernel(sizes, chunk, with_tail, table_ref, place_ref, *refs):
    rows, share = sizes
    lefts, rights, around, outs, right = refs[:4], refs[4:14], refs[14], refs[15:19], refs[19]
    slots = 4 * share
    blocks = rows * share
    width, block = right.shape[1:]
    base_at = (3 * rows + 1) * LANES
    target_at = base_at + rows * LANES
    for n in range(4):
        right[n * blocks : (n + 1) * blocks] = rights[n][...]
    for m in range(2):
        for n in range(3):
            at = (4 + 4 * m + n) * blocks
            right[at : at + blocks] = rights[4 + 3 * m + n][...]
        at = (7 + 4 * m) * blocks
        right[at : at + blocks] = around[m]
    right[12 * blocks] = jnp.zeros((width, block), right.dtype)

    half, is_low = place_ref[0], place_ref[1] == 1
    start = pl.multiple_of(half * width, width)
    slot_at = [place_ref[2 + a // share] * share + a % share for a in range(slots)]

    def bases_of(r):
        return [table_ref[base_at + r * LANES + slot_at[a]] for a in range(slots)]

    def left_at(a, r, offset, size):
        at = (r * share + a % share) * block
        return lefts[a // share][pl.ds(at + offset, size)]

    for n, r in enumerate(chunk):
        bases = bases_of(r)
        targets = [table_ref[target_at + r * LANES + slot_at[j]] for j in range(slots)]
        product = None
        for a in range(0, slots, 2):
            lines = [
                [right[table_ref[bases[a + m] + targets[j]]] for m in range(2)]
                for j in range(slots)
            ]
            stacked = jnp.concatenate([jnp.concatenate(x, axis=1) for x in lines], axis=0)
            left = jnp.concatenate([left_at(a + m, r, 0, block) for m in range(2)], axis=1)
            term = lax.dot_general(stacked, left, NT, preferred_element_type=jnp.float32)
            product = term if product is None else product + term
        for p in range(4):
            for s in range(share):
                j = p * share + s
                outs[p][(n * share + s) * width : (n * share + s + 1) * width] = product[
                    j * width : (j + 1) * width
                ].astype(jnp.bfloat16)
    if not with_tail:
        return

    z = lax.broadcasted_iota(jnp.int32, (width, block), 0) + half * width
    on_diagonal = lax.broadcasted_iota(jnp.int32, (width, block), 1) == z
    sum_values = jnp.zeros((width, block), jnp.float32)
    sum_square = jnp.zeros((width, block), jnp.float32)
    for r in range(rows):
        bases = bases_of(r)
        for a in range(slots):
            other = right[table_ref[bases[a]]]
            mine = left_at(a, r, start, width)
            sum_square += mine.astype(jnp.float32) * other.astype(jnp.float32)
        low, high = (left_at(a, r, start, width).astype(jnp.float32) for a in (share, 3 * share))
        sum_values += jnp.where(on_diagonal, jnp.where(is_low, low, high), 0.0)
    sums = [jnp.sum(s, axis=(0, 1), keepdims=True) for s in (sum_values, sum_square)]
    lane = lax.broadcasted_iota(jnp.int32, (TAIL, block), 1)
    tail = jnp.zeros((TAIL, block), jnp.float32)
    for n, rest in enumerate(sums):
        for m in range(3):
            term = rest.astype(jnp.bfloat16).astype(jnp.float32)
            tail = jnp.where(lane == 2 * m + n, term, tail)
            rest = rest - term
    for out in outs:
        out[len(chunk) * share * width :] = tail.astype(jnp.bfloat16)


def products(sizes, chunk, with_tail, table, place, lefts, rights, around):
    rows, share = sizes
    block = lefts[0].shape[1]
    width, slots = block // 2, 4 * share
    length = len(chunk) * share * width + (TAIL if with_tail else 0)
    part = jax.ShapeDtypeStruct((length, block), jnp.bfloat16)
    flops = 2 * len(chunk) * slots * slots * width * block * block
    return pl.pallas_call(
        functools.partial(product_kernel, sizes, chunk, with_tail),
        out_shape=[part] * 4,
        in_specs=[smem(), smem()] + [vmem()] * 15,
        out_specs=[vmem()] * 4,
        scratch_shapes=[
            pltpu.VMEM((12 * rows * share + 1, width, block), jnp.bfloat16),
        ],
        compiler_params=limit(32),
        cost_estimate=pl.CostEstimate(flops=flops, bytes_accessed=4 * 2**20, transcendentals=0),
        name="products",
    )(table, place, *lefts, *rights, around)


PLANE_PARTS = ((1, 3), (0, 2), (2, 0), (3, 1))


def add_kernel(fib_ref, own_ref, near_ref, mid_ref, far_ref, out_ref):
    parts = (own_ref, near_ref, mid_ref, far_ref)

    def write(*pair):
        first, second = (p[p.shape[0] - TAIL :].astype(jnp.float32) for p in pair)
        lane = lax.broadcasted_iota(jnp.int32, first.shape, 1)
        totals = []
        for n in range(2):
            terms = [
                [
                    jnp.sum(jnp.where(lane == 2 * m + n, p, 0.0), axis=1, keepdims=True)
                    for m in range(3)
                ]
                for p in (first, second)
            ]
            a, b = (t[0] + (t[1] + t[2]) for t in terms)
            totals.append(a + b)
        total = jnp.where(lane == 0, totals[0], jnp.where(lane == 1, totals[1], 0.0))
        out_ref[...] = total[:8]

    for plane, pair in enumerate(PLANE_PARTS):
        pl.when(fib_ref[0] == plane)(functools.partial(write, *(parts[n] for n in pair)))


def added(fib, parts):
    return pl.pallas_call(
        add_kernel,
        out_shape=jax.ShapeDtypeStruct((8, 128), jnp.float32),
        in_specs=[smem()] + [vmem()] * 4,
        out_specs=vmem(),
        compiler_params=limit(6),
        name="add",
    )(fib, *parts)


def join_kernel(chunks, fib_ref, *refs):
    out_ref = refs[-1]
    share, block = out_ref.shape[1:3]
    width = block // 2

    def write(*pair):
        for c, chunk in enumerate(chunks):
            for n, r in enumerate(chunk):
                for s in range(share):
                    at = (n * share + s) * width
                    halves = [refs[4 * c + p][at : at + width] for p in pair]
                    out_ref[r, s] = jnp.concatenate(halves, axis=0).T

    for plane, pair in enumerate(PLANE_PARTS):
        pl.when(fib_ref[0] == plane)(functools.partial(write, *pair))


def joined(sizes, chunks, fib, parts):
    block = parts[0].shape[1]
    return pl.pallas_call(
        functools.partial(join_kernel, chunks),
        out_shape=jax.ShapeDtypeStruct((*sizes, block, block), parts[0].dtype),
        in_specs=[smem()] + [vmem()] * len(parts),
        out_specs=vmem(),
        compiler_params=limit(8),
        name="join",
    )(fib, *parts)


def middle_body(groups, values, columns, counts):
    rows, share, block, _ = values.shape
    fib = lax.axis_index("fib")
    group = lax.axis_index(PLANE)
    high = fib >= 2

    low_order, high_order = (1, 0, 2, 3), (2, 3, 1, 0)
    inward = [[(0, 1), (3, 2)], [(1, 2), (2, 1)], [(0, 2), (3, 1)]]
    outward = [[(j, i) for i, j in pairs] for pairs in inward]

    def middle(pairs):
        return [(i * 4 + f, j * 4 + f) for i, j in pairs for f in (1, 2)]

    swap = [(i, i ^ 1) for i in range(groups)]
    skip = [((i + 2) % groups if i % 2 else (i - 2) % groups, i) for i in range(groups)]

    def from_both(array):
        first = lax.ppermute(array, PLANE, swap)
        return first, lax.ppermute(first, PLANE, skip)

    def from_both_middle(array):
        first = lax.ppermute(array, ALL, middle(swap))
        return first, lax.ppermute(first, ALL, middle(skip))

    flat = values.reshape(rows * share * block, block)
    near, mid = (lax.ppermute(flat, "fib", pairs) for pairs in inward[:2])

    half = jnp.where(high, 1, 0).astype(jnp.int32).reshape(1)
    own_half = (1 - fib % 2).astype(jnp.int32).reshape(1)
    own_turned = turned_half(own_half, flat, rows * share)
    own_around = from_both(own_turned)
    later, _ = lax.optimization_barrier((flat, own_around[0]))
    far = lax.ppermute(later, "fib", inward[2])
    far_around = lax.ppermute(packed(*own_around), "fib", inward[2])
    near_turned, mid_turned, far_turned = (
        turned_half(half, slab, rows * share) for slab in (near, mid, far)
    )
    near_around = from_both_middle(near_turned)
    mid_around = from_both_middle(mid_turned)
    rights = [own_turned, near_turned, mid_turned, far_turned]
    for n in range(2):
        rights += [own_around[n], near_around[n], mid_around[n]]

    group_ref = jnp.stack([group, jnp.where(high, 1, 0)]).astype(jnp.int32)
    table = slot_table(groups, group_ref, columns, counts, from_both)
    place = [jnp.where(high, 1, 0), jnp.where(high, 0, 1)]
    place += [jnp.where(high, h, l) for l, h in zip(low_order, high_order)]
    place = jnp.stack(place).astype(jnp.int32)
    sizes = (rows, share)
    chunks = (range(rows // 2), range(rows // 2, rows))
    gathered = []
    for n, chunk in enumerate(chunks):
        parts = products(sizes, chunk, n == 0, table, place, [flat, near, mid, far], rights, far_around)
        gathered += [parts[0]] + [
            lax.ppermute(o, "fib", pairs) for o, pairs in zip(parts[1:], outward)
        ]
    fib_ref = fib.reshape(1).astype(jnp.int32)
    sums = added(fib_ref, gathered[:4])
    square = joined(sizes, chunks, fib_ref, gathered)

    def moved(array, bits):
        return lax.ppermute(array, PLANE, [(i, i ^ bits) for i in range(groups)])

    bits = [1 << n for n in range(groups.bit_length() - 1)]
    if len(bits) % 2:
        alone = bits.pop(len(bits) // 2)
        sums = sums + moved(sums, alone)
    while bits:
        one, two = bits.pop(0), bits.pop()
        a, b, c = moved(sums, one), moved(sums, two), moved(sums, one | two)
        sums = (sums + a) + (b + c)
    return square, sums[0, :2]


def solution(mesh):
    in_specs = (P(("row", "col"), "fib", None, None), P(("row", "col"), None), P(("row", "col")))
    out_specs = (P(("row", "col"), "fib", None, None), P())
    groups = mesh.shape["row"] * mesh.shape["col"]

    def body(values, columns, counts):
        fits = groups >= 4 and groups & (groups - 1) == 0 and mesh.shape["fib"] == 4
        if fits and values.shape[0] >= BAND:
            return middle_body(groups, values, columns, counts)
        return general_body(values, columns, counts)

    return jax.shard_map(body, mesh=mesh, in_specs=in_specs, out_specs=out_specs, check_vma=False)
```

```python
import functools

import jax
import jax.numpy as jnp
from jax import lax
from jax.experimental import pallas as pl
from jax.experimental.pallas import tpu as pltpu
from jax.sharding import PartitionSpec as P

BAND = 6
PLANE = ("row", "col")
ALL = ("row", "col", "fib")
NT = (((1,), (1,)), ((), ()))


def padded(array, sides, width):
    for axis, dim in sides:
        size, length = (lax.axis_size(axis), array.shape[dim])
        up = [(i, (i + 1) % size) for i in range(size)]
        down = [(j, i) for i, j in up]
        last = lax.slice_in_dim(array, length - width, length, axis=dim)
        initial = lax.slice_in_dim(array, 0, width, axis=dim)
        before = lax.ppermute(last, axis, up)
        after = lax.ppermute(initial, axis, down)
        array = jnp.concatenate([before, array, after], axis=dim)
    return array


def band_product(
    left_tiles, left_keep, fetch_index, target_cols, target_keep, window, window_cols, window_counts
):
    picked = jnp.take(window, fetch_index, axis=0)
    picked_cols = jnp.take(window_cols, fetch_index, axis=0)
    picked_counts = jnp.take(window_counts, fetch_index, axis=0)
    alive_slots = lax.broadcasted_iota(jnp.int32, picked_cols.shape, 1) < picked_counts[:, None]
    matches = (picked_cols[:, None, :] == target_cols[None, :, None]) & alive_slots[:, None, :]
    matches = matches & left_keep[:, None, None] & target_keep[None, :, None]
    chosen = jnp.einsum(
        "ajs,asxy->ajxy", matches.astype(jnp.bfloat16), picked, preferred_element_type=jnp.float32
    ).astype(jnp.bfloat16)
    return jnp.einsum("axy,ajyz->jxz", left_tiles, chosen, preferred_element_type=jnp.float32)


def general_body(values, columns, counts):
    rows_here = values.shape[0]
    share_count = values.shape[1]
    slot_count = columns.shape[1]
    block_total = rows_here * lax.axis_size(("row", "col"))
    fib_index = lax.axis_index("fib")
    full_rows = lax.all_gather(values, "fib", axis=1, tiled=True)
    window, window_cols, window_counts = (
        padded(full_rows, ((("row", "col"), 0),), BAND),
        padded(columns, ((("row", "col"), 0),), BAND),
        padded(counts, ((("row", "col"), 0),), BAND),
    )
    local_rows = jnp.arange(rows_here, dtype=jnp.int32)
    row_ids = lax.axis_index(("row", "col")) * rows_here + local_rows
    fetch_all = (columns - row_ids[:, None] + BAND) % block_total + local_rows[:, None]
    slot_ids = jnp.arange(slot_count, dtype=jnp.int32)
    keep_mask = slot_ids[None, :] < counts[:, None]
    first_slot = fib_index * share_count

    def one_row(operands):
        return band_product(*operands, window, window_cols, window_counts)

    own_rows = lax.dynamic_slice_in_dim(window, BAND, rows_here, 0)
    target_cols = lax.dynamic_slice_in_dim(columns, first_slot, share_count, 1)
    target_keep = lax.dynamic_slice_in_dim(keep_mask, first_slot, share_count, 1)
    product = lax.map(one_row, (own_rows, keep_mask, fetch_all, target_cols, target_keep))
    is_first = (fib_index == 0).astype(jnp.float32)
    trace_values = is_first * jnp.sum(
        jnp.diagonal(values[:, 0].astype(jnp.float32), axis1=1, axis2=2)
    )
    trace_square = is_first * jnp.sum(jnp.diagonal(product[:, 0], axis1=1, axis2=2))
    traces = lax.psum(jnp.stack([trace_values, trace_square]), ("row", "col", "fib"))
    return (product.astype(jnp.bfloat16), traces)


LANES = 128
NO_SLOT = 40
TAIL = 16


def vmem():
    return pl.BlockSpec(memory_space=pltpu.VMEM)


def smem():
    return pl.BlockSpec(memory_space=pltpu.SMEM)


def limit(mebibytes):
    return pltpu.CompilerParams(vmem_limit_bytes=mebibytes * 2**20)


LOW_PLACE, HIGH_PLACE = (1, 0, 2, 3), (3, 2, 0, 1)


def turn_into(out_ref, at, blocks, in_ref, half):
    width, block = out_ref.shape[1:]
    z = lax.broadcasted_iota(jnp.int32, (width, block), 0) + half * width
    pick = (lax.broadcasted_iota(jnp.int32, (width, block), 1) == z).astype(jnp.bfloat16)
    for n in range(blocks):
        out_ref[at + n] = lax.dot_general(
            pick, in_ref[n * block : (n + 1) * block], NT, preferred_element_type=jnp.float32
        ).astype(jnp.bfloat16)


def turn_kernel(half_ref, in_ref, out_ref):
    turn_into(out_ref, 0, out_ref.shape[0], in_ref, half_ref[0])


def turned_half(half, slab, blocks):
    block = slab.shape[1]
    return pl.pallas_call(
        turn_kernel,
        out_shape=jax.ShapeDtypeStruct((blocks, block // 2, block), slab.dtype),
        in_specs=[smem(), vmem()],
        out_specs=vmem(),
        compiler_params=limit(8),
        name="turn",
    )(half, slab)


def pack_kernel(first_ref, second_ref, out_ref):
    out_ref[0] = first_ref[...]
    out_ref[1] = second_ref[...]


def packed(first, second):
    return pl.pallas_call(
        pack_kernel,
        out_shape=jax.ShapeDtypeStruct((2, *first.shape), first.dtype),
        in_specs=[vmem()] * 2,
        out_specs=vmem(),
        compiler_params=limit(8),
        name="pack",
    )(first, second)


def slots_of(group_ref, counts_ref, columns_ref, groups):
    rows, slots = columns_ref.shape
    row = lax.broadcasted_iota(jnp.int32, (rows, slots), 0)
    count = jnp.zeros((rows, slots), jnp.int32)
    for r in range(rows):
        count = jnp.where(row == r, counts_ref[r], count)
    used = lax.broadcasted_iota(jnp.int32, (rows, slots), 1) < count
    total = groups * rows
    distance = columns_ref[...] - (group_ref[0] * rows + row)
    distance = jnp.where(distance > BAND, distance - total, distance)
    distance = jnp.where(distance < -BAND, distance + total, distance)
    return row, used, distance


def find_kernel(groups, group_ref, counts_ref, columns_ref, out_ref):
    rows, slots = columns_ref.shape
    share = slots // 4
    _, used, distance = slots_of(group_ref, counts_ref, columns_ref, groups)
    at = jnp.where(used, distance + 2 * BAND, LANES)
    lane = lax.broadcasted_iota(jnp.int32, (rows, LANES), 1)
    row = lax.broadcasted_iota(jnp.int32, (rows, LANES), 0)
    found = jnp.full((rows, LANES), -1, jnp.int32)
    for s in range(slots):
        p = jnp.where(group_ref[1] == 1, HIGH_PLACE[s // share], LOW_PLACE[s // share])
        found = jnp.where(at[:, s : s + 1] == lane, (p * rows + row) * share + s % share, found)
    out_ref[...] = found


def table_kernel(groups, group_ref, counts_ref, columns_ref, own_ref, first_ref, second_ref, out_ref):
    rows, slots = columns_ref.shape
    count = slots // 4 * rows
    nothing = 12 * count
    row, used, distance = slots_of(group_ref, counts_ref, columns_ref, groups)
    out_ref[...] = jnp.full(out_ref.shape, nothing, jnp.int32)
    for n, ref in enumerate((own_ref, first_ref, second_ref)):
        found = ref[...]
        out_ref[n * rows : (n + 1) * rows] = jnp.where(
            found < 0, nothing, found + n * 4 * count
        )
    to = row + distance
    even = group_ref[0] % 2 == 0
    after = jnp.where(even, rows, 2 * rows) - rows
    before = jnp.where(even, 2 * rows, rows) + rows
    to = jnp.where(to >= rows, to + after, jnp.where(to < 0, to + before, to))
    base = to * LANES - distance + 2 * BAND
    base = jnp.where(used, base, 3 * rows * LANES + 2 * BAND)
    out_ref[3 * rows + 1 : 4 * rows + 1, :slots] = base
    out_ref[4 * rows + 1 : 5 * rows + 1, :slots] = jnp.where(used, distance, NO_SLOT)


def found_slots(groups, group, columns, counts):
    return pl.pallas_call(
        functools.partial(find_kernel, groups),
        out_shape=jax.ShapeDtypeStruct((columns.shape[0], LANES), jnp.int32),
        in_specs=[smem(), smem(), vmem()],
        out_specs=vmem(),
        compiler_params=limit(2),
        name="find",
    )(group, counts, columns)


def slot_table(groups, group, columns, counts, found, first, second):
    height = -(-(5 * columns.shape[0] + 1) // 8) * 8
    table = pl.pallas_call(
        functools.partial(table_kernel, groups),
        out_shape=jax.ShapeDtypeStruct((height, LANES), jnp.int32),
        in_specs=[smem(), smem()] + [vmem()] * 4,
        out_specs=vmem(),
        compiler_params=limit(2),
        name="table",
    )(group, counts, columns, found, first, second)
    return table.reshape(-1)


def collect(right, lefts, rights, around, half):
    blocks = rights[0].shape[0]
    for n in range(3):
        right[n * blocks : (n + 1) * blocks] = rights[n][...]
    turn_into(right, 3 * blocks, blocks, lefts[3], half)
    for m in range(2):
        for n in range(3):
            at = (4 + 4 * m + n) * blocks
            right[at : at + blocks] = rights[3 + 3 * m + n][...]
        at = (7 + 4 * m) * blocks
        right[at : at + blocks] = around[m]
    right[12 * blocks] = jnp.zeros(right.shape[1:], right.dtype)


PART_SLABS = (1, 3, 2, 0)


def product_kernel(sizes, chunk, is_first, table_ref, place_ref, *refs):
    rows, share = sizes
    lefts = refs[:4]
    if is_first:
        rights, around, outs, right = refs[4:13], refs[13], refs[14:18], refs[18]
        collect(right, lefts, rights, around, place_ref[0])
    else:
        right, earlier, outs = refs[4], refs[5:7], refs[7:11]
        for old, new in zip(earlier, outs[2:]):
            new[: old.shape[0]] = old[...]
    slots = 4 * share
    width, block = right.shape[1:]
    base_at = (3 * rows + 1) * LANES
    target_at = base_at + rows * LANES

    half, is_low = place_ref[0], place_ref[1] == 1
    start = pl.multiple_of(half * width, width)
    slot_at = [place_ref[2 + a // share] * share + a % share for a in range(slots)]

    def bases_of(r):
        return [table_ref[base_at + r * LANES + slot_at[a]] for a in range(slots)]

    def left_at(a, r, offset, size):
        at = (r * share + a % share) * block
        return lefts[a // share][pl.ds(at + offset, size)]

    for n, r in enumerate(chunk):
        bases = bases_of(r)
        targets = [table_ref[target_at + r * LANES + slot_at[j]] for j in range(slots)]
        product = None
        for a in range(0, slots, 2):
            lines = [
                [right[table_ref[bases[a + m] + targets[j]]] for m in range(2)]
                for j in range(slots)
            ]
            stacked = jnp.concatenate([jnp.concatenate(x, axis=1) for x in lines], axis=0)
            left = jnp.concatenate([left_at(a + m, r, 0, block) for m in range(2)], axis=1)
            term = lax.dot_general(stacked, left, NT, preferred_element_type=jnp.float32)
            product = term if product is None else product + term
        for p, out in zip(PART_SLABS, outs):
            at = n if p in (1, 3) or is_first else r
            for s in range(share):
                j = p * share + s
                out[(at * share + s) * width : (at * share + s + 1) * width] = product[
                    j * width : (j + 1) * width
                ].astype(jnp.bfloat16)
    if not is_first:
        return

    z = lax.broadcasted_iota(jnp.int32, (width, block), 0) + half * width
    on_diagonal = lax.broadcasted_iota(jnp.int32, (width, block), 1) == z
    sum_values = jnp.zeros((width, block), jnp.float32)
    sum_square = jnp.zeros((width, block), jnp.float32)
    for r in range(rows):
        bases = bases_of(r)
        for a in range(slots):
            other = right[table_ref[bases[a]]]
            mine = left_at(a, r, start, width)
            sum_square += mine.astype(jnp.float32) * other.astype(jnp.float32)
        low, high = (left_at(a, r, start, width).astype(jnp.float32) for a in (share, 3 * share))
        sum_values += jnp.where(on_diagonal, jnp.where(is_low, low, high), 0.0)
    sums = [jnp.sum(s, axis=(0, 1), keepdims=True) for s in (sum_values, sum_square)]
    lane = lax.broadcasted_iota(jnp.int32, (TAIL, block), 1)
    tail = jnp.zeros((TAIL, block), jnp.float32)
    for n, rest in enumerate(sums):
        for m in range(3):
            term = rest.astype(jnp.bfloat16).astype(jnp.float32)
            tail = jnp.where(lane == 2 * m + n, term, tail)
            rest = rest - term
    for out in outs[:2]:
        out[len(chunk) * share * width :] = tail.astype(jnp.bfloat16)


def products(sizes, chunk, is_first, table, place, lefts, *rest):
    rows, share = sizes
    block = lefts[0].shape[1]
    width, slots = block // 2, 4 * share
    sent = len(chunk) * share * width + (TAIL if is_first else 0)
    kept = (len(chunk) if is_first else rows) * share * width
    shapes = [(sent, block)] * 2 + [(kept, block)] * 2
    if is_first:
        shapes.append((12 * rows * share + 1, width, block))
    operands = [*lefts, *rest]
    flops = 2 * len(chunk) * slots * slots * width * block * block
    return pl.pallas_call(
        functools.partial(product_kernel, sizes, chunk, is_first),
        out_shape=[jax.ShapeDtypeStruct(shape, jnp.bfloat16) for shape in shapes],
        in_specs=[smem(), smem()] + [vmem()] * len(operands),
        out_specs=[vmem()] * len(shapes),
        compiler_params=limit(28),
        cost_estimate=pl.CostEstimate(flops=flops, bytes_accessed=4 * 2**20, transcendentals=0),
        name="products",
    )(table, place, *operands)


def add_kernel(fib_ref, near_ref, far_ref, out_ref):
    is_low = fib_ref[0] < 2
    tails = [p[p.shape[0] - TAIL :].astype(jnp.float32) for p in (near_ref, far_ref)]
    halves = jnp.where(is_low, *tails), jnp.where(is_low, *tails[::-1])
    lane = lax.broadcasted_iota(jnp.int32, halves[0].shape, 1)
    totals = []
    for n in range(2):
        terms = [
            [
                jnp.sum(jnp.where(lane == 2 * m + n, h, 0.0), axis=1, keepdims=True)
                for m in range(3)
            ]
            for h in halves
        ]
        a, b = (t[0] + (t[1] + t[2]) for t in terms)
        totals.append(a + b)
    total = jnp.where(lane == 0, totals[0], jnp.where(lane == 1, totals[1], 0.0))
    out_ref[...] = total[:8]


def added(fib, near, far):
    return pl.pallas_call(
        add_kernel,
        out_shape=jax.ShapeDtypeStruct((8, 128), jnp.float32),
        in_specs=[smem()] + [vmem()] * 2,
        out_specs=vmem(),
        compiler_params=limit(6),
        name="add",
    )(fib, near, far)


def join_kernel(chunks, fib_ref, own_ref, mid_ref, *refs):
    out_ref = refs[-1]
    share, block = out_ref.shape[1:3]
    width = block // 2

    def write(of):
        for c, chunk in enumerate(chunks):
            for n, r in enumerate(chunk):
                for s in range(share):
                    halves = [
                        ref[(at * share + s) * width : (at * share + s + 1) * width]
                        for ref, at in of(c, n, r)
                    ]
                    out_ref[r, s] = jnp.concatenate(halves, axis=0).T

    cases = (
        lambda c, n, r: ((refs[2 * c], n), (refs[2 * c + 1], n)),
        lambda c, n, r: ((own_ref, r), (mid_ref, r)),
        lambda c, n, r: ((mid_ref, r), (own_ref, r)),
        lambda c, n, r: ((refs[2 * c + 1], n), (refs[2 * c], n)),
    )
    for plane, of in enumerate(cases):
        pl.when(fib_ref[0] == plane)(functools.partial(write, of))


def joined(sizes, chunks, fib, parts):
    block = parts[0].shape[1]
    return pl.pallas_call(
        functools.partial(join_kernel, chunks),
        out_shape=jax.ShapeDtypeStruct((*sizes, block, block), parts[0].dtype),
        in_specs=[smem()] + [vmem()] * len(parts),
        out_specs=vmem(),
        compiler_params=limit(8),
        name="join",
    )(fib, *parts)


def middle_body(groups, values, columns, counts):
    rows, share, block, _ = values.shape
    fib = lax.axis_index("fib")
    group = lax.axis_index(PLANE)
    high = fib >= 2

    low_order, high_order = (1, 0, 2, 3), (2, 3, 1, 0)
    inward = [[(0, 1), (3, 2)], [(1, 2), (2, 1)], [(0, 2), (3, 1)]]
    outward = [[(j, i) for i, j in pairs] for pairs in inward]

    def middle(pairs):
        return [(i * 4 + f, j * 4 + f) for i, j in pairs for f in (1, 2)]

    swap = [(i, i ^ 1) for i in range(groups)]
    skip = [((i + 2) % groups if i % 2 else (i - 2) % groups, i) for i in range(groups)]

    def from_both_middle(array, *before):
        first = lax.ppermute(array, ALL, middle(swap))
        passed, *_ = lax.optimization_barrier((first, *before))
        return first, lax.ppermute(passed, ALL, middle(skip))

    flat = values.reshape(rows * share * block, block)
    near, mid = (lax.ppermute(flat, "fib", pairs) for pairs in inward[:2])

    half = jnp.where(high, 1, 0).astype(jnp.int32).reshape(1)
    own_half = (1 - fib % 2).astype(jnp.int32).reshape(1)
    own_turned = turned_half(own_half, flat, rows * share)
    own_first = lax.ppermute(own_turned, PLANE, swap)
    group_ref = jnp.stack([group, jnp.where(high, 1, 0)]).astype(jnp.int32)
    found = found_slots(groups, group_ref, columns, counts)
    found_first = lax.ppermute(found, PLANE, swap)
    later, own_passed, found_passed = lax.optimization_barrier((flat, own_first, found_first))
    own_second = lax.ppermute(own_passed, PLANE, skip)
    found_second = lax.ppermute(found_passed, PLANE, skip)
    far = lax.ppermute(later, "fib", inward[2])
    own_first, own_second, found_second = lax.optimization_barrier(
        (own_first, own_second, found_second)
    )
    far_around = lax.ppermute(packed(own_first, own_second), "fib", inward[2])
    table = slot_table(groups, group_ref, columns, counts, found, found_first, found_second)
    near_turned, mid_turned = (turned_half(half, slab, rows * share) for slab in (near, mid))
    near_around = from_both_middle(near_turned, table)
    mid_around = from_both_middle(mid_turned)
    rights = [own_turned, near_turned, mid_turned]
    rights += [own_first, near_around[0], mid_around[0]]
    rights += [own_second, near_around[1], mid_around[1]]

    place = [jnp.where(high, 1, 0), jnp.where(high, 0, 1)]
    place += [jnp.where(high, h, l) for l, h in zip(low_order, high_order)]
    place = jnp.stack(place).astype(jnp.int32)
    sizes = (rows, share)
    chunks = (range(rows // 2), range(rows // 2, rows))
    lefts = [flat, near, mid, far]

    def sent(part, n):
        return lax.ppermute(part, "fib", outward[n])

    near_part, far_part, mid_part, own_part, right = products(
        sizes, chunks[0], True, table, place, lefts, *rights, far_around
    )
    parts = [sent(far_part, 2), sent(near_part, 0)][::-1]
    near_part, far_part, mid_part, own_part = products(
        sizes, chunks[1], False, table, place, lefts, right, mid_part, own_part
    )
    parts += [sent(far_part, 2), sent(near_part, 0)][::-1]
    mid_part = sent(mid_part, 1)
    fib_ref = fib.reshape(1).astype(jnp.int32)
    square = joined(sizes, chunks, fib_ref, [own_part, mid_part, *parts])

    def moved(array, bits):
        pairs = [(i * 4 + f, (i ^ bits) * 4 + f) for i in range(groups) for f in (0, 3)]
        return lax.ppermute(array, ALL, pairs)

    sums = added(fib_ref, *parts[:2])
    bits = [1 << n for n in range(groups.bit_length() - 1)]
    if len(bits) % 2:
        alone = bits.pop(len(bits) // 2)
        sums = sums + moved(sums, alone)
    while bits:
        one, two = bits.pop(0), bits.pop()
        a, b, c = moved(sums, one), moved(sums, two), moved(sums, one | two)
        sums = (sums + a) + (b + c)
    back = lax.ppermute(sums, "fib", inward[0])
    sums = jnp.where((fib == 1) | (fib == 2), back, sums)
    return square, sums[0, :2]


def solution(mesh):
    in_specs = (P(("row", "col"), "fib", None, None), P(("row", "col"), None), P(("row", "col")))
    out_specs = (P(("row", "col"), "fib", None, None), P())
    groups = mesh.shape["row"] * mesh.shape["col"]

    def body(values, columns, counts):
        fits = groups >= 4 and groups & (groups - 1) == 0 and mesh.shape["fib"] == 4
        if fits and values.shape[0] >= BAND:
            return middle_body(groups, values, columns, counts)
        return general_body(values, columns, counts)

    return jax.shard_map(body, mesh=mesh, in_specs=in_specs, out_specs=out_specs, check_vma=False)
```

```python
import functools

import jax
import jax.numpy as jnp
from jax import lax
from jax.experimental import pallas as pl
from jax.experimental.pallas import tpu as pltpu
from jax.sharding import PartitionSpec as P

BAND = 6
PLANE = ("row", "col")
ALL = ("row", "col", "fib")
NT = (((1,), (1,)), ((), ()))


def padded(array, sides, width):
    for axis, dim in sides:
        size, length = (lax.axis_size(axis), array.shape[dim])
        up = [(i, (i + 1) % size) for i in range(size)]
        down = [(j, i) for i, j in up]
        last = lax.slice_in_dim(array, length - width, length, axis=dim)
        initial = lax.slice_in_dim(array, 0, width, axis=dim)
        before = lax.ppermute(last, axis, up)
        after = lax.ppermute(initial, axis, down)
        array = jnp.concatenate([before, array, after], axis=dim)
    return array


def band_product(
    left_tiles, left_keep, fetch_index, target_cols, target_keep, window, window_cols, window_counts
):
    picked = jnp.take(window, fetch_index, axis=0)
    picked_cols = jnp.take(window_cols, fetch_index, axis=0)
    picked_counts = jnp.take(window_counts, fetch_index, axis=0)
    alive_slots = lax.broadcasted_iota(jnp.int32, picked_cols.shape, 1) < picked_counts[:, None]
    matches = (picked_cols[:, None, :] == target_cols[None, :, None]) & alive_slots[:, None, :]
    matches = matches & left_keep[:, None, None] & target_keep[None, :, None]
    chosen = jnp.einsum(
        "ajs,asxy->ajxy", matches.astype(jnp.bfloat16), picked, preferred_element_type=jnp.float32
    ).astype(jnp.bfloat16)
    return jnp.einsum("axy,ajyz->jxz", left_tiles, chosen, preferred_element_type=jnp.float32)


def general_body(values, columns, counts):
    rows_here = values.shape[0]
    share_count = values.shape[1]
    slot_count = columns.shape[1]
    block_total = rows_here * lax.axis_size(("row", "col"))
    fib_index = lax.axis_index("fib")
    full_rows = lax.all_gather(values, "fib", axis=1, tiled=True)
    window, window_cols, window_counts = (
        padded(full_rows, ((("row", "col"), 0),), BAND),
        padded(columns, ((("row", "col"), 0),), BAND),
        padded(counts, ((("row", "col"), 0),), BAND),
    )
    local_rows = jnp.arange(rows_here, dtype=jnp.int32)
    row_ids = lax.axis_index(("row", "col")) * rows_here + local_rows
    fetch_all = (columns - row_ids[:, None] + BAND) % block_total + local_rows[:, None]
    slot_ids = jnp.arange(slot_count, dtype=jnp.int32)
    keep_mask = slot_ids[None, :] < counts[:, None]
    first_slot = fib_index * share_count

    def one_row(operands):
        return band_product(*operands, window, window_cols, window_counts)

    own_rows = lax.dynamic_slice_in_dim(window, BAND, rows_here, 0)
    target_cols = lax.dynamic_slice_in_dim(columns, first_slot, share_count, 1)
    target_keep = lax.dynamic_slice_in_dim(keep_mask, first_slot, share_count, 1)
    product = lax.map(one_row, (own_rows, keep_mask, fetch_all, target_cols, target_keep))
    is_first = (fib_index == 0).astype(jnp.float32)
    trace_values = is_first * jnp.sum(
        jnp.diagonal(values[:, 0].astype(jnp.float32), axis1=1, axis2=2)
    )
    trace_square = is_first * jnp.sum(jnp.diagonal(product[:, 0], axis1=1, axis2=2))
    traces = lax.psum(jnp.stack([trace_values, trace_square]), ("row", "col", "fib"))
    return (product.astype(jnp.bfloat16), traces)


LANES = 128
NO_SLOT = 40
TAIL = 16


def vmem():
    return pl.BlockSpec(memory_space=pltpu.VMEM)


def smem():
    return pl.BlockSpec(memory_space=pltpu.SMEM)


def limit(mebibytes):
    return pltpu.CompilerParams(vmem_limit_bytes=mebibytes * 2**20)


LOW_PLACE, HIGH_PLACE = (1, 0, 2, 3), (3, 2, 0, 1)


def turn_into(out_ref, at, blocks, in_ref, half):
    block = in_ref.shape[1]
    width = block // 2
    z = lax.broadcasted_iota(jnp.int32, (width, block), 0) + half * width
    pick = (lax.broadcasted_iota(jnp.int32, (width, block), 1) == z).astype(jnp.bfloat16)
    for n in range(blocks):
        out_ref[at + n * width : at + (n + 1) * width] = lax.dot_general(
            pick, in_ref[n * block : (n + 1) * block], NT, preferred_element_type=jnp.float32
        ).astype(jnp.bfloat16)


def turn_kernel(half_ref, in_ref, out_ref):
    turn_into(out_ref, 0, in_ref.shape[0] // in_ref.shape[1], in_ref, half_ref[0])


def turned_half(half, slab):
    return pl.pallas_call(
        turn_kernel,
        out_shape=jax.ShapeDtypeStruct((slab.shape[0] // 2, slab.shape[1]), slab.dtype),
        in_specs=[smem(), vmem()],
        out_specs=vmem(),
        compiler_params=limit(8),
        name="turn",
    )(half, slab)


def pack_kernel(first_ref, second_ref, out_ref):
    size = out_ref.shape[0] // 2
    out_ref[:size] = first_ref[:size]
    out_ref[size:] = second_ref[:size]


def packed(first, second):
    size = 2 * first.shape[0]
    return pl.pallas_call(
        pack_kernel,
        out_shape=jax.ShapeDtypeStruct((size, first.shape[1]), first.dtype),
        in_specs=[vmem()] * 2,
        out_specs=vmem(),
        compiler_params=limit(8),
        name="pack",
    )(first, second)


def slots_of(group_ref, counts_ref, columns_ref, groups):
    rows, slots = columns_ref.shape
    row = lax.broadcasted_iota(jnp.int32, (rows, slots), 0)
    count = jnp.zeros((rows, slots), jnp.int32)
    for r in range(rows):
        count = jnp.where(row == r, counts_ref[r], count)
    used = lax.broadcasted_iota(jnp.int32, (rows, slots), 1) < count
    total = groups * rows
    distance = columns_ref[...] - (group_ref[0] * rows + row)
    distance = jnp.where(distance > BAND, distance - total, distance)
    distance = jnp.where(distance < -BAND, distance + total, distance)
    return row, used, distance


def find_kernel(groups, group_ref, counts_ref, columns_ref, out_ref):
    rows, slots = columns_ref.shape
    share = slots // 4
    _, used, distance = slots_of(group_ref, counts_ref, columns_ref, groups)
    at = jnp.where(used, distance + 2 * BAND, LANES)
    lane = lax.broadcasted_iota(jnp.int32, (rows, LANES), 1)
    row = lax.broadcasted_iota(jnp.int32, (rows, LANES), 0)
    found = jnp.full((rows, LANES), -1, jnp.int32)
    for s in range(slots):
        p = jnp.where(group_ref[1] == 1, HIGH_PLACE[s // share], LOW_PLACE[s // share])
        found = jnp.where(at[:, s : s + 1] == lane, (p * rows + row) * share + s % share, found)
    out_ref[...] = found


def found_slots(groups, group, columns, counts):
    return pl.pallas_call(
        functools.partial(find_kernel, groups),
        out_shape=jax.ShapeDtypeStruct((columns.shape[0], LANES), jnp.int32),
        in_specs=[smem(), smem(), vmem()],
        out_specs=vmem(),
        compiler_params=limit(2),
        name="find",
    )(group, counts, columns)


def table_kernel(groups, group_ref, counts_ref, columns_ref, own_ref, first_ref, second_ref, out_ref):
    rows, slots = columns_ref.shape
    count = slots // 4 * rows
    nothing = 12 * count
    row, used, distance = slots_of(group_ref, counts_ref, columns_ref, groups)
    out_ref[...] = jnp.full(out_ref.shape, nothing, jnp.int32)
    for n, ref in enumerate((own_ref, first_ref, second_ref)):
        found = ref[...]
        out_ref[n * rows : (n + 1) * rows] = jnp.where(
            found < 0, nothing, found + n * 4 * count
        )
    to = row + distance
    even = group_ref[0] % 2 == 0
    after = jnp.where(even, rows, 2 * rows) - rows
    before = jnp.where(even, 2 * rows, rows) + rows
    to = jnp.where(to >= rows, to + after, jnp.where(to < 0, to + before, to))
    base = to * LANES - distance + 2 * BAND
    base = jnp.where(used, base, 3 * rows * LANES + 2 * BAND)
    out_ref[3 * rows + 1 : 4 * rows + 1, :slots] = base
    out_ref[4 * rows + 1 : 5 * rows + 1, :slots] = jnp.where(used, distance, NO_SLOT)


def slot_table(groups, group, counts, columns, own, first, second):
    height = -(-(5 * columns.shape[0] + 1) // 8) * 8
    table = pl.pallas_call(
        functools.partial(table_kernel, groups),
        out_shape=jax.ShapeDtypeStruct((height, LANES), jnp.int32),
        in_specs=[smem(), smem()] + [vmem()] * 4,
        out_specs=vmem(),
        compiler_params=limit(6),
        name="table",
    )(group, counts, columns, own, first, second)
    return table.reshape(-1)


def collect(right, rights, around, turned):
    size = turned.shape[0]
    for n, ref in enumerate(rights):
        at = (n + n // 3) * size
        right[at : at + size] = ref[:size]
    right[3 * size : 4 * size] = turned[...]
    for m in range(2):
        right[(7 + 4 * m) * size : (8 + 4 * m) * size] = around[m * size : (m + 1) * size]
    rest = right.shape[0] - 12 * size
    right[12 * size :] = jnp.zeros((rest, right.shape[1]), right.dtype)


PARTS = (0, 3, 1, 2)


def product_kernel(sizes, chunk, is_first, table_ref, place_ref, *refs):
    rows, share = sizes
    lefts, rights, around, turned = refs[:4], refs[4:13], refs[13], refs[14]
    outs, right = refs[15:19], refs[19]
    slots = 4 * share
    block = right.shape[1]
    width = block // 2
    base_at = (3 * rows + 1) * LANES
    target_at = base_at + rows * LANES
    collect(right, rights, around, turned)

    def half_at(index):
        return right[pl.ds(pl.multiple_of(index * width, width), width)]

    half, is_low = place_ref[0], place_ref[1] == 1
    start = pl.multiple_of(half * width, width)
    slot_at = [place_ref[2 + a // share] * share + a % share for a in range(slots)]

    def bases_of(r):
        return [table_ref[base_at + r * LANES + slot_at[a]] for a in range(slots)]

    def left_at(a, r, offset, size):
        at = (r * share + a % share) * block
        return lefts[a // share][pl.ds(at + offset, size)]

    for n, r in enumerate(chunk):
        bases = bases_of(r)
        targets = [table_ref[target_at + r * LANES + slot_at[j]] for j in range(slots)]
        product = None
        for a in range(0, slots, 2):
            lines = [
                [half_at(table_ref[bases[a + m] + targets[j]]) for m in range(2)]
                for j in range(slots)
            ]
            stacked = jnp.concatenate([jnp.concatenate(x, axis=1) for x in lines], axis=0)
            left = jnp.concatenate([left_at(a + m, r, 0, block) for m in range(2)], axis=1)
            term = lax.dot_general(stacked, left, NT, preferred_element_type=jnp.float32)
            product = term if product is None else product + term
        for p, out in zip(PARTS, outs):
            for s in range(share):
                j = p * share + s
                out[(n * share + s) * width : (n * share + s + 1) * width] = product[
                    j * width : (j + 1) * width
                ].astype(jnp.bfloat16)
    if not is_first:
        return

    z = lax.broadcasted_iota(jnp.int32, (width, block), 0) + half * width
    on_diagonal = lax.broadcasted_iota(jnp.int32, (width, block), 1) == z
    sum_values = jnp.zeros((width, block), jnp.float32)
    sum_square = jnp.zeros((width, block), jnp.float32)
    for r in range(rows):
        bases = bases_of(r)
        for a in range(slots):
            other = half_at(table_ref[bases[a]])
            mine = left_at(a, r, start, width)
            sum_square += mine.astype(jnp.float32) * other.astype(jnp.float32)
        low, high = (left_at(a, r, start, width).astype(jnp.float32) for a in (share, 3 * share))
        sum_values += jnp.where(on_diagonal, jnp.where(is_low, low, high), 0.0)
    sums = [jnp.sum(s, axis=(0, 1), keepdims=True) for s in (sum_values, sum_square)]
    lane = lax.broadcasted_iota(jnp.int32, (TAIL, block), 1)
    tail = jnp.zeros((TAIL, block), jnp.float32)
    for n, rest in enumerate(sums):
        for m in range(3):
            term = rest.astype(jnp.bfloat16).astype(jnp.float32)
            tail = jnp.where(lane == 2 * m + n, term, tail)
            rest = rest - term
    for out in outs:
        out[len(chunk) * share * width :] = tail.astype(jnp.bfloat16)


def products(sizes, chunk, is_first, table, place, lefts, *rest):
    rows, share = sizes
    block = lefts[0].shape[1]
    width, slots = block // 2, 4 * share
    length = len(chunk) * share * width + (TAIL if is_first else 0)
    shapes = [(length, block)] * 4
    operands = [*lefts, *rest]
    flops = 2 * len(chunk) * slots * slots * width * block * block
    return pl.pallas_call(
        functools.partial(product_kernel, sizes, chunk, is_first),
        out_shape=[jax.ShapeDtypeStruct(shape, jnp.bfloat16) for shape in shapes],
        in_specs=[smem(), smem()] + [vmem()] * len(operands),
        out_specs=[vmem()] * len(shapes),
        scratch_shapes=[pltpu.VMEM(((12 * rows * share + 1) * width, block), jnp.bfloat16)],
        compiler_params=limit(32),
        cost_estimate=pl.CostEstimate(flops=flops, bytes_accessed=4 * 2**20, transcendentals=0),
        name="products",
    )(table, place, *operands)


PLANE_PARTS = ((2, 1), (0, 3), (3, 0), (1, 2))


def add_kernel(fib_ref, own_ref, far_ref, near_ref, mid_ref, out_ref):
    parts = (own_ref, far_ref, near_ref, mid_ref)

    def write(*pair):
        first, second = (p[p.shape[0] - TAIL :].astype(jnp.float32) for p in pair)
        lane = lax.broadcasted_iota(jnp.int32, first.shape, 1)
        totals = []
        for n in range(2):
            terms = [
                [
                    jnp.sum(jnp.where(lane == 2 * m + n, p, 0.0), axis=1, keepdims=True)
                    for m in range(3)
                ]
                for p in (first, second)
            ]
            a, b = (t[0] + (t[1] + t[2]) for t in terms)
            totals.append(a + b)
        total = jnp.where(lane == 0, totals[0], jnp.where(lane == 1, totals[1], 0.0))
        out_ref[...] = total[:8]

    for plane, pair in enumerate(PLANE_PARTS):
        pl.when(fib_ref[0] == plane)(functools.partial(write, *(parts[n] for n in pair)))


def added(fib, parts):
    return pl.pallas_call(
        add_kernel,
        out_shape=jax.ShapeDtypeStruct((8, 128), jnp.float32),
        in_specs=[smem()] + [vmem()] * 4,
        out_specs=vmem(),
        compiler_params=limit(6),
        name="add",
    )(fib, *parts)


def join_kernel(chunks, fib_ref, *refs):
    out_ref = refs[-1]
    share, block = out_ref.shape[1:3]
    width = block // 2

    def write(*pair):
        for c, chunk in enumerate(chunks):
            for n, r in enumerate(chunk):
                for s in range(share):
                    at = (n * share + s) * width
                    halves = [refs[4 * c + p][at : at + width] for p in pair]
                    out_ref[r, s] = jnp.concatenate(halves, axis=0).T

    for plane, pair in enumerate(PLANE_PARTS):
        pl.when(fib_ref[0] == plane)(functools.partial(write, *pair))


def joined(sizes, chunks, fib, parts):
    block = parts[0].shape[1]
    return pl.pallas_call(
        functools.partial(join_kernel, chunks),
        out_shape=jax.ShapeDtypeStruct((*sizes, block, block), parts[0].dtype),
        in_specs=[smem()] + [vmem()] * len(parts),
        out_specs=vmem(),
        compiler_params=limit(8),
        name="join",
    )(fib, *parts)


def middle_body(groups, values, columns, counts):
    rows, share, block, _ = values.shape
    fib = lax.axis_index("fib")
    group = lax.axis_index(PLANE)
    high = fib >= 2

    low_order, high_order = (1, 0, 2, 3), (2, 3, 1, 0)
    inward = [[(0, 1), (3, 2)], [(1, 2), (2, 1)], [(0, 2), (3, 1)]]
    outward = [[(j, i) for i, j in pairs] for pairs in inward]

    def middle(pairs):
        return [(i * 4 + f, j * 4 + f) for i, j in pairs for f in (1, 2)]

    swap = [(i, i ^ 1) for i in range(groups)]
    skip = [((i + 2) % groups if i % 2 else (i - 2) % groups, i) for i in range(groups)]

    def from_both_middle(array, *before):
        first = lax.ppermute(array, ALL, middle(swap))
        passed, *_ = lax.optimization_barrier((first, *before))
        return first, lax.ppermute(passed, ALL, middle(skip))

    flat = values.reshape(rows * share * block, block)
    near, mid = (lax.ppermute(flat, "fib", pairs) for pairs in inward[:2])

    half = jnp.where(high, 1, 0).astype(jnp.int32)
    own_half = (1 - fib % 2).astype(jnp.int32)
    own = turned_half(own_half.reshape(1), flat)
    own_first = lax.ppermute(own, PLANE, swap)
    own_second = lax.ppermute(own_first, PLANE, skip)
    later, *_ = lax.optimization_barrier((flat, own_first))
    far = lax.ppermute(later, "fib", inward[2])
    far_around = lax.ppermute(packed(own_first, own_second), "fib", inward[2])
    near_turned, mid_turned, far_turned = (
        turned_half(half.reshape(1), slab) for slab in (near, mid, far)
    )
    group_ref = jnp.stack([group, half]).astype(jnp.int32)
    found = found_slots(groups, group_ref, columns, counts)
    found_first = lax.ppermute(found, PLANE, swap)
    found_second = lax.ppermute(found_first, PLANE, skip)
    table = slot_table(groups, group_ref, counts, columns, found, found_first, found_second)
    near_around = from_both_middle(near_turned)
    mid_around = from_both_middle(mid_turned)
    rights = [own, near_turned, mid_turned]
    rights += [own_first, near_around[0], mid_around[0]]
    rights += [own_second, near_around[1], mid_around[1]]

    place = [half, 1 - half]
    place += [jnp.where(high, h, l) for l, h in zip(low_order, high_order)]
    place = jnp.stack(place).astype(jnp.int32)
    sizes = (rows, share)
    chunks = (range(rows // 2), range(rows // 2, rows))
    gathered = []
    lefts, rest = [flat, near, mid, far], [*rights, far_around, far_turned]
    for n, chunk in enumerate(chunks):
        own_part, *parts = products(sizes, chunk, n == 0, table, place, lefts, *rest)
        gathered.append(own_part)
        gathered += [
            lax.ppermute(part, "fib", outward[m - 1]) for m, part in zip(PARTS[1:], parts)
        ]
    fib_ref = fib.reshape(1).astype(jnp.int32)
    sums = added(fib_ref, gathered[:4])
    square = joined(sizes, chunks, fib_ref, gathered)

    def moved(array, bits):
        return lax.ppermute(array, PLANE, [(i, i ^ bits) for i in range(groups)])

    bits = [1 << n for n in range(groups.bit_length() - 1)]
    if len(bits) % 2:
        alone = bits.pop(len(bits) // 2)
        sums = sums + moved(sums, alone)
    while bits:
        one, two = bits.pop(0), bits.pop()
        a, b, c = moved(sums, one), moved(sums, two), moved(sums, one | two)
        sums = (sums + a) + (b + c)
    return square, sums[0, :2]


def solution(mesh):
    in_specs = (P(("row", "col"), "fib", None, None), P(("row", "col"), None), P(("row", "col")))
    out_specs = (P(("row", "col"), "fib", None, None), P())
    groups = mesh.shape["row"] * mesh.shape["col"]

    def body(values, columns, counts):
        rows, share = values.shape[:2]
        fits = groups >= 4 and groups & (groups - 1) == 0 and mesh.shape["fib"] == 4
        if fits and BAND <= rows <= TAIL and rows * share <= 64:
            return middle_body(groups, values, columns, counts)
        return general_body(values, columns, counts)

    return jax.shard_map(body, mesh=mesh, in_specs=in_specs, out_specs=out_specs, check_vma=False)
```

```python
import functools

import jax
import jax.numpy as jnp
from jax import lax
from jax.experimental import pallas as pl
from jax.experimental.pallas import tpu as pltpu
from jax.sharding import PartitionSpec as P

BAND = 6
PLANE = ("row", "col")
ALL = ("row", "col", "fib")
NT = (((1,), (1,)), ((), ()))


def padded(array, sides, width):
    for axis, dim in sides:
        size, length = (lax.axis_size(axis), array.shape[dim])
        up = [(i, (i + 1) % size) for i in range(size)]
        down = [(j, i) for i, j in up]
        last = lax.slice_in_dim(array, length - width, length, axis=dim)
        initial = lax.slice_in_dim(array, 0, width, axis=dim)
        before = lax.ppermute(last, axis, up)
        after = lax.ppermute(initial, axis, down)
        array = jnp.concatenate([before, array, after], axis=dim)
    return array


def band_product(
    left_tiles, left_keep, fetch_index, target_cols, target_keep, window, window_cols, window_counts
):
    picked = jnp.take(window, fetch_index, axis=0)
    picked_cols = jnp.take(window_cols, fetch_index, axis=0)
    picked_counts = jnp.take(window_counts, fetch_index, axis=0)
    alive_slots = lax.broadcasted_iota(jnp.int32, picked_cols.shape, 1) < picked_counts[:, None]
    matches = (picked_cols[:, None, :] == target_cols[None, :, None]) & alive_slots[:, None, :]
    matches = matches & left_keep[:, None, None] & target_keep[None, :, None]
    chosen = jnp.einsum(
        "ajs,asxy->ajxy", matches.astype(jnp.bfloat16), picked, preferred_element_type=jnp.float32
    ).astype(jnp.bfloat16)
    return jnp.einsum("axy,ajyz->jxz", left_tiles, chosen, preferred_element_type=jnp.float32)


def general_body(values, columns, counts):
    rows_here = values.shape[0]
    share_count = values.shape[1]
    slot_count = columns.shape[1]
    block_total = rows_here * lax.axis_size(("row", "col"))
    fib_index = lax.axis_index("fib")
    full_rows = lax.all_gather(values, "fib", axis=1, tiled=True)
    window, window_cols, window_counts = (
        padded(full_rows, ((("row", "col"), 0),), BAND),
        padded(columns, ((("row", "col"), 0),), BAND),
        padded(counts, ((("row", "col"), 0),), BAND),
    )
    local_rows = jnp.arange(rows_here, dtype=jnp.int32)
    row_ids = lax.axis_index(("row", "col")) * rows_here + local_rows
    fetch_all = (columns - row_ids[:, None] + BAND) % block_total + local_rows[:, None]
    slot_ids = jnp.arange(slot_count, dtype=jnp.int32)
    keep_mask = slot_ids[None, :] < counts[:, None]
    first_slot = fib_index * share_count

    def one_row(operands):
        return band_product(*operands, window, window_cols, window_counts)

    own_rows = lax.dynamic_slice_in_dim(window, BAND, rows_here, 0)
    target_cols = lax.dynamic_slice_in_dim(columns, first_slot, share_count, 1)
    target_keep = lax.dynamic_slice_in_dim(keep_mask, first_slot, share_count, 1)
    product = lax.map(one_row, (own_rows, keep_mask, fetch_all, target_cols, target_keep))
    is_first = (fib_index == 0).astype(jnp.float32)
    trace_values = is_first * jnp.sum(
        jnp.diagonal(values[:, 0].astype(jnp.float32), axis1=1, axis2=2)
    )
    trace_square = is_first * jnp.sum(jnp.diagonal(product[:, 0], axis1=1, axis2=2))
    traces = lax.psum(jnp.stack([trace_values, trace_square]), ("row", "col", "fib"))
    return (product.astype(jnp.bfloat16), traces)


LANES = 128
NO_SLOT = 40
TAIL = 16


def vmem():
    return pl.BlockSpec(memory_space=pltpu.VMEM)


def smem():
    return pl.BlockSpec(memory_space=pltpu.SMEM)


def limit(mebibytes):
    return pltpu.CompilerParams(vmem_limit_bytes=mebibytes * 2**20)


LOW_PLACE, HIGH_PLACE = (1, 0, 2, 3), (3, 2, 0, 1)


def turn_into(out_ref, at, blocks, in_ref, half):
    block = in_ref.shape[1]
    width = block // 2
    z = lax.broadcasted_iota(jnp.int32, (width, block), 0) + half * width
    pick = (lax.broadcasted_iota(jnp.int32, (width, block), 1) == z).astype(jnp.bfloat16)
    for n in range(blocks):
        out_ref[at + n * width : at + (n + 1) * width] = lax.dot_general(
            pick, in_ref[n * block : (n + 1) * block], NT, preferred_element_type=jnp.float32
        ).astype(jnp.bfloat16)


def turn_kernel(half_ref, in_ref, out_ref):
    turn_into(out_ref, 0, in_ref.shape[0] // in_ref.shape[1], in_ref, half_ref[0])


def turned_half(half, slab):
    return pl.pallas_call(
        turn_kernel,
        out_shape=jax.ShapeDtypeStruct((slab.shape[0] // 2, slab.shape[1]), slab.dtype),
        in_specs=[smem(), vmem()],
        out_specs=vmem(),
        compiler_params=limit(8),
        name="turn",
    )(half, slab)


def pack_kernel(first_ref, second_ref, out_ref):
    size = out_ref.shape[0] // 2
    out_ref[:size] = first_ref[:size]
    out_ref[size:] = second_ref[:size]


def packed(first, second):
    size = 2 * first.shape[0]
    return pl.pallas_call(
        pack_kernel,
        out_shape=jax.ShapeDtypeStruct((size, first.shape[1]), first.dtype),
        in_specs=[vmem()] * 2,
        out_specs=vmem(),
        compiler_params=limit(8),
        name="pack",
    )(first, second)


def slots_of(group_ref, counts_ref, columns_ref, groups):
    rows, slots = columns_ref.shape
    row = lax.broadcasted_iota(jnp.int32, (rows, slots), 0)
    count = jnp.zeros((rows, slots), jnp.int32)
    for r in range(rows):
        count = jnp.where(row == r, counts_ref[r], count)
    used = lax.broadcasted_iota(jnp.int32, (rows, slots), 1) < count
    total = groups * rows
    distance = columns_ref[...] - (group_ref[0] * rows + row)
    distance = jnp.where(distance > BAND, distance - total, distance)
    distance = jnp.where(distance < -BAND, distance + total, distance)
    return row, used, distance


def find_kernel(groups, group_ref, counts_ref, columns_ref, out_ref):
    rows, slots = columns_ref.shape
    share = slots // 4
    _, used, distance = slots_of(group_ref, counts_ref, columns_ref, groups)
    at = jnp.where(used, distance + 2 * BAND, LANES)
    lane = lax.broadcasted_iota(jnp.int32, (rows, LANES), 1)
    row = lax.broadcasted_iota(jnp.int32, (rows, LANES), 0)
    found = jnp.full((rows, LANES), -1, jnp.int32)
    for s in range(slots):
        p = jnp.where(group_ref[1] == 1, HIGH_PLACE[s // share], LOW_PLACE[s // share])
        found = jnp.where(at[:, s : s + 1] == lane, (p * rows + row) * share + s % share, found)
    out_ref[...] = found


def found_slots(groups, group, columns, counts):
    return pl.pallas_call(
        functools.partial(find_kernel, groups),
        out_shape=jax.ShapeDtypeStruct((columns.shape[0], LANES), jnp.int32),
        in_specs=[smem(), smem(), vmem()],
        out_specs=vmem(),
        compiler_params=limit(2),
        name="find",
    )(group, counts, columns)


def table_kernel(groups, group_ref, counts_ref, columns_ref, own_ref, first_ref, second_ref, out_ref):
    rows, slots = columns_ref.shape
    count = slots // 4 * rows
    nothing = 12 * count
    row, used, distance = slots_of(group_ref, counts_ref, columns_ref, groups)
    out_ref[...] = jnp.full(out_ref.shape, nothing, jnp.int32)
    for n, ref in enumerate((own_ref, first_ref, second_ref)):
        found = ref[...]
        out_ref[n * rows : (n + 1) * rows] = jnp.where(
            found < 0, nothing, found + n * 4 * count
        )
    to = row + distance
    even = group_ref[0] % 2 == 0
    after = jnp.where(even, rows, 2 * rows) - rows
    before = jnp.where(even, 2 * rows, rows) + rows
    to = jnp.where(to >= rows, to + after, jnp.where(to < 0, to + before, to))
    base = to * LANES - distance + 2 * BAND
    base = jnp.where(used, base, 3 * rows * LANES + 2 * BAND)
    out_ref[3 * rows + 1 : 4 * rows + 1, :slots] = base
    out_ref[4 * rows + 1 : 5 * rows + 1, :slots] = jnp.where(used, distance, NO_SLOT)


def slot_table(groups, group, counts, columns, own, first, second):
    height = -(-(5 * columns.shape[0] + 1) // 8) * 8
    table = pl.pallas_call(
        functools.partial(table_kernel, groups),
        out_shape=jax.ShapeDtypeStruct((height, LANES), jnp.int32),
        in_specs=[smem(), smem()] + [vmem()] * 4,
        out_specs=vmem(),
        compiler_params=limit(6),
        name="table",
    )(group, counts, columns, own, first, second)
    return table.reshape(-1)


def collect(right, rights, around, turned):
    size = turned.shape[0]
    for n, ref in enumerate(rights):
        at = (n + n // 3) * size
        right[at : at + size] = ref[:size]
    right[3 * size : 4 * size] = turned[...]
    for m in range(2):
        right[(7 + 4 * m) * size : (8 + 4 * m) * size] = around[m * size : (m + 1) * size]
    rest = right.shape[0] - 12 * size
    right[12 * size :] = jnp.zeros((rest, right.shape[1]), right.dtype)


PARTS = (0, 3, 1, 2)


def product_kernel(sizes, chunk, is_first, table_ref, place_ref, *refs):
    rows, share = sizes
    lefts, rights, around, turned = refs[:4], refs[4:13], refs[13], refs[14]
    outs, right = refs[15:19], refs[19]
    slots = 4 * share
    block = right.shape[1]
    width = block // 2
    base_at = (3 * rows + 1) * LANES
    target_at = base_at + rows * LANES
    collect(right, rights, around, turned)

    def half_at(index):
        return right[pl.ds(pl.multiple_of(index * width, width), width)]

    half, is_low = place_ref[0], place_ref[1] == 1
    start = pl.multiple_of(half * width, width)
    slot_at = [place_ref[2 + a // share] * share + a % share for a in range(slots)]

    def bases_of(r):
        return [table_ref[base_at + r * LANES + slot_at[a]] for a in range(slots)]

    def left_at(a, r, offset, size):
        at = (r * share + a % share) * block
        return lefts[a // share][pl.ds(at + offset, size)]

    for n, r in enumerate(chunk):
        bases = bases_of(r)
        targets = [table_ref[target_at + r * LANES + slot_at[j]] for j in range(slots)]
        product = None
        for a in range(0, slots, 2):
            lines = [
                [half_at(table_ref[bases[a + m] + targets[j]]) for m in range(2)]
                for j in range(slots)
            ]
            stacked = jnp.concatenate([jnp.concatenate(x, axis=1) for x in lines], axis=0)
            left = jnp.concatenate([left_at(a + m, r, 0, block) for m in range(2)], axis=1)
            term = lax.dot_general(stacked, left, NT, preferred_element_type=jnp.float32)
            product = term if product is None else product + term
        for p, out in zip(PARTS, outs):
            for s in range(share):
                j = p * share + s
                out[(n * share + s) * width : (n * share + s + 1) * width] = product[
                    j * width : (j + 1) * width
                ].astype(jnp.bfloat16)
    if not is_first:
        return

    z = lax.broadcasted_iota(jnp.int32, (width, block), 0) + half * width
    on_diagonal = lax.broadcasted_iota(jnp.int32, (width, block), 1) == z
    sum_values = jnp.zeros((width, block), jnp.float32)
    sum_square = jnp.zeros((width, block), jnp.float32)
    for r in range(rows):
        bases = bases_of(r)
        for a in range(slots):
            other = half_at(table_ref[bases[a]])
            mine = left_at(a, r, start, width)
            sum_square += mine.astype(jnp.float32) * other.astype(jnp.float32)
        low, high = (left_at(a, r, start, width).astype(jnp.float32) for a in (share, 3 * share))
        sum_values += jnp.where(on_diagonal, jnp.where(is_low, low, high), 0.0)
    sums = [jnp.sum(s, axis=(0, 1), keepdims=True) for s in (sum_values, sum_square)]
    lane = lax.broadcasted_iota(jnp.int32, (TAIL, block), 1)
    tail = jnp.zeros((TAIL, block), jnp.float32)
    for n, rest in enumerate(sums):
        for m in range(3):
            term = rest.astype(jnp.bfloat16).astype(jnp.float32)
            tail = jnp.where(lane == 2 * m + n, term, tail)
            rest = rest - term
    for out in outs:
        out[len(chunk) * share * width :] = tail.astype(jnp.bfloat16)


def products(sizes, chunk, is_first, table, place, lefts, *rest):
    rows, share = sizes
    block = lefts[0].shape[1]
    width, slots = block // 2, 4 * share
    length = len(chunk) * share * width + (TAIL if is_first else 0)
    shapes = [(length, block)] * 4
    operands = [*lefts, *rest]
    flops = 2 * len(chunk) * slots * slots * width * block * block
    return pl.pallas_call(
        functools.partial(product_kernel, sizes, chunk, is_first),
        out_shape=[jax.ShapeDtypeStruct(shape, jnp.bfloat16) for shape in shapes],
        in_specs=[smem(), smem()] + [vmem()] * len(operands),
        out_specs=[vmem()] * len(shapes),
        scratch_shapes=[pltpu.VMEM(((12 * rows * share + 1) * width, block), jnp.bfloat16)],
        compiler_params=limit(32),
        cost_estimate=pl.CostEstimate(flops=flops, bytes_accessed=4 * 2**20, transcendentals=0),
        name="products",
    )(table, place, *operands)


PLANE_PARTS = ((2, 1), (0, 3), (3, 0), (1, 2))


def add_kernel(fib_ref, own_ref, far_ref, near_ref, mid_ref, out_ref):
    parts = (own_ref, far_ref, near_ref, mid_ref)

    def write(*pair):
        first, second = (p[p.shape[0] - TAIL :].astype(jnp.float32) for p in pair)
        lane = lax.broadcasted_iota(jnp.int32, first.shape, 1)
        totals = []
        for n in range(2):
            terms = [
                [
                    jnp.sum(jnp.where(lane == 2 * m + n, p, 0.0), axis=1, keepdims=True)
                    for m in range(3)
                ]
                for p in (first, second)
            ]
            a, b = (t[0] + (t[1] + t[2]) for t in terms)
            totals.append(a + b)
        total = jnp.where(lane == 0, totals[0], jnp.where(lane == 1, totals[1], 0.0))
        out_ref[...] = total[:8]

    for plane, pair in enumerate(PLANE_PARTS):
        pl.when(fib_ref[0] == plane)(functools.partial(write, *(parts[n] for n in pair)))


def added(fib, parts):
    return pl.pallas_call(
        add_kernel,
        out_shape=jax.ShapeDtypeStruct((8, 128), jnp.float32),
        in_specs=[smem()] + [vmem()] * 4,
        out_specs=vmem(),
        compiler_params=limit(6),
        name="add",
    )(fib, *parts)


def join_kernel(chunks, fib_ref, *refs):
    out_ref = refs[-1]
    share, block = out_ref.shape[1:3]
    width = block // 2

    def write(*pair):
        for c, chunk in enumerate(chunks):
            for n, r in enumerate(chunk):
                for s in range(share):
                    at = (n * share + s) * width
                    halves = [refs[4 * c + p][at : at + width] for p in pair]
                    out_ref[r, s] = jnp.concatenate(halves, axis=0).T

    for plane, pair in enumerate(PLANE_PARTS):
        pl.when(fib_ref[0] == plane)(functools.partial(write, *pair))


def joined(sizes, chunks, fib, parts):
    block = parts[0].shape[1]
    return pl.pallas_call(
        functools.partial(join_kernel, chunks),
        out_shape=jax.ShapeDtypeStruct((*sizes, block, block), parts[0].dtype),
        in_specs=[smem()] + [vmem()] * len(parts),
        out_specs=vmem(),
        compiler_params=limit(8),
        name="join",
    )(fib, *parts)


def middle_body(groups, values, columns, counts):
    rows, share, block, _ = values.shape
    fib = lax.axis_index("fib")
    group = lax.axis_index(PLANE)
    high = fib >= 2

    low_order, high_order = (1, 0, 2, 3), (2, 3, 1, 0)
    inward = [[(0, 1), (3, 2)], [(1, 2), (2, 1)], [(0, 2), (3, 1)]]
    outward = [[(j, i) for i, j in pairs] for pairs in inward]

    def middle(pairs):
        return [(i * 4 + f, j * 4 + f) for i, j in pairs for f in (1, 2)]

    swap = [(i, i ^ 1) for i in range(groups)]
    skip = [((i + 2) % groups if i % 2 else (i - 2) % groups, i) for i in range(groups)]

    def from_both_middle(array, *before):
        first = lax.ppermute(array, ALL, middle(swap))
        passed, *_ = lax.optimization_barrier((first, *before))
        return first, lax.ppermute(passed, ALL, middle(skip))

    flat = values.reshape(rows * share * block, block)
    near, mid = (lax.ppermute(flat, "fib", pairs) for pairs in inward[:2])

    half = jnp.where(high, 1, 0).astype(jnp.int32)
    own_half = (1 - fib % 2).astype(jnp.int32)
    own = turned_half(own_half.reshape(1), flat)
    own_first = lax.ppermute(own, PLANE, swap)
    group_ref = jnp.stack([group, half]).astype(jnp.int32)
    found = found_slots(groups, group_ref, columns, counts)
    found_first = lax.ppermute(found, PLANE, swap)
    own_passed, _ = lax.optimization_barrier((own_first, found_first))
    own_second = lax.ppermute(own_passed, PLANE, skip)
    later, *_ = lax.optimization_barrier((flat, own_first))
    far = lax.ppermute(later, "fib", inward[2])
    near_turned, mid_turned, far_turned = (
        turned_half(half.reshape(1), slab) for slab in (near, mid, far)
    )
    found_second = lax.ppermute(found_first, PLANE, skip)
    first, second, *_ = lax.optimization_barrier((own_first, own_second, found_second))
    far_around = lax.ppermute(packed(first, second), "fib", inward[2])
    table = slot_table(groups, group_ref, counts, columns, found, found_first, found_second)
    near_around = from_both_middle(near_turned)
    mid_around = from_both_middle(mid_turned)
    rights = [own, near_turned, mid_turned]
    rights += [own_first, near_around[0], mid_around[0]]
    rights += [own_second, near_around[1], mid_around[1]]

    place = [half, 1 - half]
    place += [jnp.where(high, h, l) for l, h in zip(low_order, high_order)]
    place = jnp.stack(place).astype(jnp.int32)
    sizes = (rows, share)
    chunks = (range(rows // 2), range(rows // 2, rows))
    gathered = []
    lefts, rest = [flat, near, mid, far], [*rights, far_around, far_turned]
    for n, chunk in enumerate(chunks):
        own_part, *parts = products(sizes, chunk, n == 0, table, place, lefts, *rest)
        gathered.append(own_part)
        gathered += [
            lax.ppermute(part, "fib", outward[m - 1]) for m, part in zip(PARTS[1:], parts)
        ]
    fib_ref = fib.reshape(1).astype(jnp.int32)
    sums = added(fib_ref, gathered[:4])
    square = joined(sizes, chunks, fib_ref, gathered)

    def moved(array, bits):
        return lax.ppermute(array, PLANE, [(i, i ^ bits) for i in range(groups)])

    bits = [1 << n for n in range(groups.bit_length() - 1)]
    if len(bits) % 2:
        alone = bits.pop(len(bits) // 2)
        sums = sums + moved(sums, alone)
    while bits:
        one, two = bits.pop(0), bits.pop()
        a, b, c = moved(sums, one), moved(sums, two), moved(sums, one | two)
        sums = (sums + a) + (b + c)
    return square, sums[0, :2]


def solution(mesh):
    in_specs = (P(("row", "col"), "fib", None, None), P(("row", "col"), None), P(("row", "col")))
    out_specs = (P(("row", "col"), "fib", None, None), P())
    groups = mesh.shape["row"] * mesh.shape["col"]

    def body(values, columns, counts):
        rows, share = values.shape[:2]
        fits = groups >= 4 and groups & (groups - 1) == 0 and mesh.shape["fib"] == 4
        if fits and BAND <= rows <= TAIL and rows * share <= 64:
            return middle_body(groups, values, columns, counts)
        return general_body(values, columns, counts)

    return jax.shard_map(body, mesh=mesh, in_specs=in_specs, out_specs=out_specs, check_vma=False)
```

```python
import functools

import jax
import jax.numpy as jnp
from jax import lax
from jax.experimental import pallas as pl
from jax.experimental.pallas import tpu as pltpu
from jax.sharding import PartitionSpec as P

BAND = 6
PLANE = ("row", "col")
ALL = ("row", "col", "fib")
NT = (((1,), (1,)), ((), ()))


def padded(array, sides, width):
    for axis, dim in sides:
        size, length = (lax.axis_size(axis), array.shape[dim])
        up = [(i, (i + 1) % size) for i in range(size)]
        down = [(j, i) for i, j in up]
        last = lax.slice_in_dim(array, length - width, length, axis=dim)
        initial = lax.slice_in_dim(array, 0, width, axis=dim)
        before = lax.ppermute(last, axis, up)
        after = lax.ppermute(initial, axis, down)
        array = jnp.concatenate([before, array, after], axis=dim)
    return array


def band_product(
    left_tiles, left_keep, fetch_index, target_cols, target_keep, window, window_cols, window_counts
):
    picked = jnp.take(window, fetch_index, axis=0)
    picked_cols = jnp.take(window_cols, fetch_index, axis=0)
    picked_counts = jnp.take(window_counts, fetch_index, axis=0)
    alive_slots = lax.broadcasted_iota(jnp.int32, picked_cols.shape, 1) < picked_counts[:, None]
    matches = (picked_cols[:, None, :] == target_cols[None, :, None]) & alive_slots[:, None, :]
    matches = matches & left_keep[:, None, None] & target_keep[None, :, None]
    chosen = jnp.einsum(
        "ajs,asxy->ajxy", matches.astype(jnp.bfloat16), picked, preferred_element_type=jnp.float32
    ).astype(jnp.bfloat16)
    return jnp.einsum("axy,ajyz->jxz", left_tiles, chosen, preferred_element_type=jnp.float32)


def general_body(values, columns, counts):
    rows_here = values.shape[0]
    share_count = values.shape[1]
    slot_count = columns.shape[1]
    block_total = rows_here * lax.axis_size(("row", "col"))
    fib_index = lax.axis_index("fib")
    full_rows = lax.all_gather(values, "fib", axis=1, tiled=True)
    window, window_cols, window_counts = (
        padded(full_rows, ((("row", "col"), 0),), BAND),
        padded(columns, ((("row", "col"), 0),), BAND),
        padded(counts, ((("row", "col"), 0),), BAND),
    )
    local_rows = jnp.arange(rows_here, dtype=jnp.int32)
    row_ids = lax.axis_index(("row", "col")) * rows_here + local_rows
    fetch_all = (columns - row_ids[:, None] + BAND) % block_total + local_rows[:, None]
    slot_ids = jnp.arange(slot_count, dtype=jnp.int32)
    keep_mask = slot_ids[None, :] < counts[:, None]
    first_slot = fib_index * share_count

    def one_row(operands):
        return band_product(*operands, window, window_cols, window_counts)

    own_rows = lax.dynamic_slice_in_dim(window, BAND, rows_here, 0)
    target_cols = lax.dynamic_slice_in_dim(columns, first_slot, share_count, 1)
    target_keep = lax.dynamic_slice_in_dim(keep_mask, first_slot, share_count, 1)
    product = lax.map(one_row, (own_rows, keep_mask, fetch_all, target_cols, target_keep))
    is_first = (fib_index == 0).astype(jnp.float32)
    trace_values = is_first * jnp.sum(
        jnp.diagonal(values[:, 0].astype(jnp.float32), axis1=1, axis2=2)
    )
    trace_square = is_first * jnp.sum(jnp.diagonal(product[:, 0], axis1=1, axis2=2))
    traces = lax.psum(jnp.stack([trace_values, trace_square]), ("row", "col", "fib"))
    return (product.astype(jnp.bfloat16), traces)


LANES = 128
NO_SLOT = 40
TAIL = 16


def vmem():
    return pl.BlockSpec(memory_space=pltpu.VMEM)


def smem():
    return pl.BlockSpec(memory_space=pltpu.SMEM)


def limit(mebibytes):
    return pltpu.CompilerParams(vmem_limit_bytes=mebibytes * 2**20)


LOW_PLACE, HIGH_PLACE = (1, 0, 2, 3), (3, 2, 0, 1)


def turn_into(out_ref, at, blocks, in_ref, half):
    block = in_ref.shape[1]
    width = block // 2
    z = lax.broadcasted_iota(jnp.int32, (width, block), 0) + half * width
    pick = (lax.broadcasted_iota(jnp.int32, (width, block), 1) == z).astype(jnp.bfloat16)
    for n in range(blocks):
        out_ref[at + n * width : at + (n + 1) * width] = lax.dot_general(
            pick, in_ref[n * block : (n + 1) * block], NT, preferred_element_type=jnp.float32
        ).astype(jnp.bfloat16)


def turn_kernel(half_ref, in_ref, out_ref):
    turn_into(out_ref, 0, in_ref.shape[0] // in_ref.shape[1], in_ref, half_ref[0])


def turned_half(half, slab):
    return pl.pallas_call(
        turn_kernel,
        out_shape=jax.ShapeDtypeStruct((slab.shape[0] // 2, slab.shape[1]), slab.dtype),
        in_specs=[smem(), vmem()],
        out_specs=vmem(),
        compiler_params=limit(8),
        name="turn",
    )(half, slab)


def pack_kernel(first_ref, second_ref, out_ref):
    size = out_ref.shape[0] // 2
    out_ref[:size] = first_ref[:size]
    out_ref[size:] = second_ref[:size]


def packed(first, second):
    size = 2 * first.shape[0]
    return pl.pallas_call(
        pack_kernel,
        out_shape=jax.ShapeDtypeStruct((size, first.shape[1]), first.dtype),
        in_specs=[vmem()] * 2,
        out_specs=vmem(),
        compiler_params=limit(8),
        name="pack",
    )(first, second)


def slots_of(group_ref, counts_ref, columns_ref, groups):
    rows, slots = columns_ref.shape
    row = lax.broadcasted_iota(jnp.int32, (rows, slots), 0)
    count = jnp.zeros((rows, slots), jnp.int32)
    for r in range(rows):
        count = jnp.where(row == r, counts_ref[r], count)
    used = lax.broadcasted_iota(jnp.int32, (rows, slots), 1) < count
    total = groups * rows
    distance = columns_ref[...] - (group_ref[0] * rows + row)
    distance = jnp.where(distance > BAND, distance - total, distance)
    distance = jnp.where(distance < -BAND, distance + total, distance)
    return row, used, distance


def find_kernel(groups, group_ref, counts_ref, columns_ref, out_ref):
    rows, slots = columns_ref.shape
    share = slots // 4
    _, used, distance = slots_of(group_ref, counts_ref, columns_ref, groups)
    at = jnp.where(used, distance + 2 * BAND, LANES)
    lane = lax.broadcasted_iota(jnp.int32, (rows, LANES), 1)
    row = lax.broadcasted_iota(jnp.int32, (rows, LANES), 0)
    found = jnp.full((rows, LANES), -1, jnp.int32)
    for s in range(slots):
        p = jnp.where(group_ref[1] == 1, HIGH_PLACE[s // share], LOW_PLACE[s // share])
        found = jnp.where(at[:, s : s + 1] == lane, (p * rows + row) * share + s % share, found)
    out_ref[...] = found


def found_slots(groups, group, columns, counts):
    return pl.pallas_call(
        functools.partial(find_kernel, groups),
        out_shape=jax.ShapeDtypeStruct((columns.shape[0], LANES), jnp.int32),
        in_specs=[smem(), smem(), vmem()],
        out_specs=vmem(),
        compiler_params=limit(2),
        name="find",
    )(group, counts, columns)


def table_kernel(groups, group_ref, counts_ref, columns_ref, own_ref, first_ref, second_ref, out_ref):
    rows, slots = columns_ref.shape
    count = slots // 4 * rows
    nothing = 12 * count
    row, used, distance = slots_of(group_ref, counts_ref, columns_ref, groups)
    out_ref[...] = jnp.full(out_ref.shape, nothing, jnp.int32)
    for n, ref in enumerate((own_ref, first_ref, second_ref)):
        found = ref[...]
        out_ref[n * rows : (n + 1) * rows] = jnp.where(
            found < 0, nothing, found + n * 4 * count
        )
    to = row + distance
    even = group_ref[0] % 2 == 0
    after = jnp.where(even, rows, 2 * rows) - rows
    before = jnp.where(even, 2 * rows, rows) + rows
    to = jnp.where(to >= rows, to + after, jnp.where(to < 0, to + before, to))
    base = to * LANES - distance + 2 * BAND
    base = jnp.where(used, base, 3 * rows * LANES + 2 * BAND)
    out_ref[3 * rows + 1 : 4 * rows + 1, :slots] = base
    out_ref[4 * rows + 1 : 5 * rows + 1, :slots] = jnp.where(used, distance, NO_SLOT)


def slot_table(groups, group, counts, columns, own, first, second):
    height = -(-(5 * columns.shape[0] + 1) // 8) * 8
    table = pl.pallas_call(
        functools.partial(table_kernel, groups),
        out_shape=jax.ShapeDtypeStruct((height, LANES), jnp.int32),
        in_specs=[smem(), smem()] + [vmem()] * 4,
        out_specs=vmem(),
        compiler_params=limit(6),
        name="table",
    )(group, counts, columns, own, first, second)
    return table.reshape(-1)


def collect(right, rights, around, turned):
    size = turned.shape[0]
    for n, ref in enumerate(rights):
        at = (n + n // 3) * size
        right[at : at + size] = ref[:size]
    right[3 * size : 4 * size] = turned[...]
    for m in range(2):
        right[(7 + 4 * m) * size : (8 + 4 * m) * size] = around[m * size : (m + 1) * size]
    rest = right.shape[0] - 12 * size
    right[12 * size :] = jnp.zeros((rest, right.shape[1]), right.dtype)


PARTS = (0, 3, 1, 2)


def product_kernel(sizes, chunk, is_first, table_ref, place_ref, *refs):
    rows, share = sizes
    lefts, rights, around, turned = refs[:4], refs[4:13], refs[13], refs[14]
    outs, right = refs[15:19], refs[19]
    slots = 4 * share
    block = right.shape[1]
    width = block // 2
    base_at = (3 * rows + 1) * LANES
    target_at = base_at + rows * LANES
    collect(right, rights, around, turned)

    def half_at(index):
        return right[pl.ds(pl.multiple_of(index * width, width), width)]

    half, is_low = place_ref[0], place_ref[1] == 1
    start = pl.multiple_of(half * width, width)
    slot_at = [place_ref[2 + a // share] * share + a % share for a in range(slots)]

    def bases_of(r):
        return [table_ref[base_at + r * LANES + slot_at[a]] for a in range(slots)]

    def left_at(a, r, offset, size):
        at = (r * share + a % share) * block
        return lefts[a // share][pl.ds(at + offset, size)]

    for n, r in enumerate(chunk):
        bases = bases_of(r)
        targets = [table_ref[target_at + r * LANES + slot_at[j]] for j in range(slots)]
        product = None
        for a in range(0, slots, 2):
            lines = [
                [half_at(table_ref[bases[a + m] + targets[j]]) for m in range(2)]
                for j in range(slots)
            ]
            stacked = jnp.concatenate([jnp.concatenate(x, axis=1) for x in lines], axis=0)
            left = jnp.concatenate([left_at(a + m, r, 0, block) for m in range(2)], axis=1)
            term = lax.dot_general(stacked, left, NT, preferred_element_type=jnp.float32)
            product = term if product is None else product + term
        for p, out in zip(PARTS, outs):
            for s in range(share):
                j = p * share + s
                out[(n * share + s) * width : (n * share + s + 1) * width] = product[
                    j * width : (j + 1) * width
                ].astype(jnp.bfloat16)
    if not is_first:
        return

    z = lax.broadcasted_iota(jnp.int32, (width, block), 0) + half * width
    on_diagonal = lax.broadcasted_iota(jnp.int32, (width, block), 1) == z
    sum_values = jnp.zeros((width, block), jnp.float32)
    sum_square = jnp.zeros((width, block), jnp.float32)
    for r in range(rows):
        bases = bases_of(r)
        for a in range(slots):
            other = half_at(table_ref[bases[a]])
            mine = left_at(a, r, start, width)
            sum_square += mine.astype(jnp.float32) * other.astype(jnp.float32)
        low, high = (left_at(a, r, start, width).astype(jnp.float32) for a in (share, 3 * share))
        sum_values += jnp.where(on_diagonal, jnp.where(is_low, low, high), 0.0)
    sums = [jnp.sum(s, axis=(0, 1), keepdims=True) for s in (sum_values, sum_square)]
    lane = lax.broadcasted_iota(jnp.int32, (TAIL, block), 1)
    tail = jnp.zeros((TAIL, block), jnp.float32)
    for n, rest in enumerate(sums):
        for m in range(3):
            term = rest.astype(jnp.bfloat16).astype(jnp.float32)
            tail = jnp.where(lane == 2 * m + n, term, tail)
            rest = rest - term
    for out in outs:
        out[len(chunk) * share * width :] = tail.astype(jnp.bfloat16)


def products(sizes, chunk, is_first, table, place, lefts, *rest):
    rows, share = sizes
    block = lefts[0].shape[1]
    width, slots = block // 2, 4 * share
    length = len(chunk) * share * width + (TAIL if is_first else 0)
    shapes = [(length, block)] * 4
    operands = [*lefts, *rest]
    flops = 2 * len(chunk) * slots * slots * width * block * block
    return pl.pallas_call(
        functools.partial(product_kernel, sizes, chunk, is_first),
        out_shape=[jax.ShapeDtypeStruct(shape, jnp.bfloat16) for shape in shapes],
        in_specs=[smem(), smem()] + [vmem()] * len(operands),
        out_specs=[vmem()] * len(shapes),
        scratch_shapes=[pltpu.VMEM(((12 * rows * share + 1) * width, block), jnp.bfloat16)],
        compiler_params=limit(32),
        cost_estimate=pl.CostEstimate(flops=flops, bytes_accessed=4 * 2**20, transcendentals=0),
        name="products",
    )(table, place, *operands)


PLANE_PARTS = ((2, 1), (0, 3), (3, 0), (1, 2))


def add_kernel(fib_ref, own_ref, far_ref, near_ref, mid_ref, out_ref):
    parts = (own_ref, far_ref, near_ref, mid_ref)

    def write(*pair):
        first, second = (p[p.shape[0] - TAIL :].astype(jnp.float32) for p in pair)
        lane = lax.broadcasted_iota(jnp.int32, first.shape, 1)
        totals = []
        for n in range(2):
            terms = [
                [
                    jnp.sum(jnp.where(lane == 2 * m + n, p, 0.0), axis=1, keepdims=True)
                    for m in range(3)
                ]
                for p in (first, second)
            ]
            a, b = (t[0] + (t[1] + t[2]) for t in terms)
            totals.append(a + b)
        total = jnp.where(lane == 0, totals[0], jnp.where(lane == 1, totals[1], 0.0))
        out_ref[...] = total[:8]

    for plane, pair in enumerate(PLANE_PARTS):
        pl.when(fib_ref[0] == plane)(functools.partial(write, *(parts[n] for n in pair)))


def added(fib, parts):
    return pl.pallas_call(
        add_kernel,
        out_shape=jax.ShapeDtypeStruct((8, 128), jnp.float32),
        in_specs=[smem()] + [vmem()] * 4,
        out_specs=vmem(),
        compiler_params=limit(6),
        name="add",
    )(fib, *parts)


def join_kernel(chunks, fib_ref, *refs):
    out_ref = refs[-1]
    share, block = out_ref.shape[1:3]
    width = block // 2

    def write(*pair):
        for c, chunk in enumerate(chunks):
            for n, r in enumerate(chunk):
                for s in range(share):
                    at = (n * share + s) * width
                    halves = [refs[4 * c + p][at : at + width] for p in pair]
                    out_ref[r, s] = jnp.concatenate(halves, axis=0).T

    for plane, pair in enumerate(PLANE_PARTS):
        pl.when(fib_ref[0] == plane)(functools.partial(write, *pair))


def joined(sizes, chunks, fib, parts):
    block = parts[0].shape[1]
    return pl.pallas_call(
        functools.partial(join_kernel, chunks),
        out_shape=jax.ShapeDtypeStruct((*sizes, block, block), parts[0].dtype),
        in_specs=[smem()] + [vmem()] * len(parts),
        out_specs=vmem(),
        compiler_params=limit(8),
        name="join",
    )(fib, *parts)


def middle_body(groups, values, columns, counts):
    rows, share, block, _ = values.shape
    fib = lax.axis_index("fib")
    group = lax.axis_index(PLANE)
    high = fib >= 2

    low_order, high_order = (1, 0, 2, 3), (2, 3, 1, 0)
    inward = [[(0, 1), (3, 2)], [(1, 2), (2, 1)], [(0, 2), (3, 1)]]
    outward = [[(j, i) for i, j in pairs] for pairs in inward]

    def middle(pairs):
        return [(i * 4 + f, j * 4 + f) for i, j in pairs for f in (1, 2)]

    swap = [(i, i ^ 1) for i in range(groups)]
    skip = [((i + 2) % groups if i % 2 else (i - 2) % groups, i) for i in range(groups)]

    def from_both_middle(array, *before):
        first = lax.ppermute(array, ALL, middle(swap))
        passed, *_ = lax.optimization_barrier((first, *before))
        return first, lax.ppermute(passed, ALL, middle(skip))

    flat = values.reshape(rows * share * block, block)
    near, mid = (lax.ppermute(flat, "fib", pairs) for pairs in inward[:2])

    half = jnp.where(high, 1, 0).astype(jnp.int32)
    own_half = (1 - fib % 2).astype(jnp.int32)
    own = turned_half(own_half.reshape(1), flat)
    own_first = lax.ppermute(own, PLANE, swap)
    group_ref = jnp.stack([group, half]).astype(jnp.int32)
    found = found_slots(groups, group_ref, columns, counts)
    found_first = lax.ppermute(found, PLANE, swap)
    own_passed, _ = lax.optimization_barrier((own_first, found_first))
    own_second = lax.ppermute(own_passed, PLANE, skip)
    later, *_ = lax.optimization_barrier((flat, own_first))
    far = lax.ppermute(later, "fib", inward[2])
    near_turned, mid_turned, far_turned = (
        turned_half(half.reshape(1), slab) for slab in (near, mid, far)
    )
    found_passed, _ = lax.optimization_barrier((found_first, own_second))
    found_second = lax.ppermute(found_passed, PLANE, skip)
    first, second, *_ = lax.optimization_barrier((own_first, own_second, found_second))
    far_around = lax.ppermute(packed(first, second), "fib", inward[2])
    table = slot_table(groups, group_ref, counts, columns, found, found_first, found_second)
    near_around = from_both_middle(near_turned)
    mid_around = from_both_middle(mid_turned)
    rights = [own, near_turned, mid_turned]
    rights += [own_first, near_around[0], mid_around[0]]
    rights += [own_second, near_around[1], mid_around[1]]

    place = [half, 1 - half]
    place += [jnp.where(high, h, l) for l, h in zip(low_order, high_order)]
    place = jnp.stack(place).astype(jnp.int32)
    sizes = (rows, share)
    chunks = (range(rows // 2), range(rows // 2, rows))
    gathered = []
    lefts, rest = [flat, near, mid, far], [*rights, far_around, far_turned]
    for n, chunk in enumerate(chunks):
        own_part, *parts = products(sizes, chunk, n == 0, table, place, lefts, *rest)
        gathered.append(own_part)
        gathered += [
            lax.ppermute(part, "fib", outward[m - 1]) for m, part in zip(PARTS[1:], parts)
        ]
    fib_ref = fib.reshape(1).astype(jnp.int32)
    sums = added(fib_ref, gathered[:4])
    square = joined(sizes, chunks, fib_ref, gathered)

    def moved(array, bits):
        return lax.ppermute(array, PLANE, [(i, i ^ bits) for i in range(groups)])

    bits = [1 << n for n in range(groups.bit_length() - 1)]
    if len(bits) % 2:
        alone = bits.pop(len(bits) // 2)
        sums = sums + moved(sums, alone)
    while bits:
        one, two = bits.pop(0), bits.pop()
        a, b, c = moved(sums, one), moved(sums, two), moved(sums, one | two)
        sums = (sums + a) + (b + c)
    return square, sums[0, :2]


def solution(mesh):
    in_specs = (P(("row", "col"), "fib", None, None), P(("row", "col"), None), P(("row", "col")))
    out_specs = (P(("row", "col"), "fib", None, None), P())
    groups = mesh.shape["row"] * mesh.shape["col"]

    def body(values, columns, counts):
        rows, share = values.shape[:2]
        fits = groups >= 4 and groups & (groups - 1) == 0 and mesh.shape["fib"] == 4
        if fits and BAND <= rows <= TAIL and rows * share <= 64:
            return middle_body(groups, values, columns, counts)
        return general_body(values, columns, counts)

    return jax.shard_map(body, mesh=mesh, in_specs=in_specs, out_specs=out_specs, check_vma=False)
```
